256 devices in a mesh: expert: 32 (over y, z), context: 8 (over x, core).
Axes of the slice: x: 4, y: 4, z: 8, core: 2. Of those that a mesh axis runs over, the one named last changes fastest.
Arguments:
- tokens: bfloat16 [32, 1024, 2048], P('expert', 'context'), may hold values from -6 to 6
- route: int32 [32, 1024, 1], P('expert'), may hold values from 0 to 31; in each aligned block of 128 rows (0 to 127, 128 to 255, ..., all dimensions but the last counted through in order) at most 8 rows name the same one
- w_inner: bfloat16 [32, 2048, 2, 4096], P('expert', None, None, 'context'), may hold values from -0.125 to 0.125
- w_state: bfloat16 [32, 2048, 128], P('expert'), may hold values from -0.015625 to 0.015625
- w_step: bfloat16 [32, 2048, 64], P('expert', None, 'context'), may hold values from -0.125 to 0.125
- step_bias: float32 [64], P('context'), may hold values from -2 to 0.5
- decay_log: float32 [64], P('context'), may hold values from -7 to -2.5
- skip_gain: float32 [64], P('context'), may hold values from 0.5 to 1.5
- conv_weight: float32 [4, 4096], P(None, 'context'), may hold values from -3 to 3
- conv_bias: float32 [4096], P('context'), may hold values from -1.5 to 1.5
- w_out: bfloat16 [32, 4096, 2048], P('expert', 'context'), may hold values from -0.09375 to 0.09375
Outputs:
- mixed: bfloat16 [32, 1024, 2048], P('expert', 'context')
The draws below stay inside these ranges and needn't reach their ends.
Inputs may be any that keep to these rules, and one draw needn't show every extreme that they name: `route`: in each aligned block of 128 positions (the rows of one device) no expert is named more than 8 times, a bound that some block reaches.
All inputs are finite; a program needn't handle non-finite values.
Results may differ from the reference program's by a relative error of at most 0.014.
Values may be sent and summed in bfloat16 or wider, within the bound.
A program may use at most 128 MiB of HBM per device.

```python
import math
import jax
import jax.numpy as jnp
import numpy as np
from jax import lax

D = 2048
DI = 4096
NSTATE = 64
HEAD_DIM = 64
CONV = 4
TOK_DEV = 128
EXPERTS = 32
SEQS = 32
SEQLEN = 1024
HEADS = 64
CAP = 8
N_CONTEXT = 8


def steps_of(stream_key, shape, cuts, smallest, high):
    level, own = 1.0, jax.random.fold_in(stream_key, 6)
    for position, blocks in cuts:
        draws = jnp.exp(jax.random.uniform(jax.random.fold_in(own, position), (blocks,), jnp.float32, smallest / len(cuts), high / len(cuts)))
        level = level * jnp.repeat(draws, shape[position] // blocks).reshape([-1 if axis == position else 1 for axis in range(len(shape))])
    return level


def routed_block(rng, own, number, rows, amount, top, most, lean):
    sequence = jax.random.permutation(rng, amount)
    heavy_load, ordinary = load_shares(amount, rows * top, most, lean, True), load_shares(amount, rows * top, most, lean, False)
    places = jnp.arange(amount)

    def named(lengths, rotation):
        used = int((lengths > 0).sum())
        fixed = max(1, used // 4)
        moved = fixed + (places - fixed + rotation * (used - fixed)) % max(1, amount - fixed)
        return jnp.zeros((amount,), jnp.int32).at[sequence[jnp.where(places < fixed, places, moved)]].set(jnp.asarray(lengths, jnp.int32))

    lengths = jnp.where(number % 4 == 0, named(heavy_load, number // 4), named(ordinary, number - number // 4 - 1))
    mixed = jax.random.permutation(jax.random.fold_in(own, 3), amount)
    source_of, sink = mixed[0:amount // 2 * 2:2], mixed[1:amount // 2 * 2:2]
    slack = jnp.minimum(lengths[source_of] - 1, most - lengths[sink]) // 2
    slack = jnp.where((source_of == sequence[0]) | (sink == sequence[0]) | (lengths[sink] == 0), 0, jnp.maximum(slack, 0))
    moved = jax.random.randint(jax.random.fold_in(own, 4), (amount // 2,), 0, 1 << 20) % (slack + 1)
    lengths = lengths.at[source_of].add(-moved).at[sink].add(moved)
    members = jnp.searchsorted(jnp.cumsum(lengths), jnp.arange(rows * top), side="right").astype(jnp.int32)
    table = members.reshape(top, rows).T
    table = table[jax.random.permutation(jax.random.fold_in(own, 1), rows)]
    rotation = jax.random.randint(jax.random.fold_in(own, 2), (rows, 1), 0, top)
    return jnp.take_along_axis(table, (jnp.arange(top)[None, :] + rotation) % top, axis=1)


def load_shares(count, total, most, skew, full):
    loads = [(1 << 20) // math.isqrt(rank ** skew) + 1 for rank in range(1, count + 1)]
    largest = most if full else min(most, max(-(-total // count), total * loads[0] // sum(loads)))
    least = 1 if total - largest >= count - 1 else 0
    holding, spare = [largest] + [least] * (count - 1), total - largest - least * (count - 1)
    while spare > 0:
        candidates = [i for i in range(1, count) if holding[i] < largest] or [i for i in range(1, count) if holding[i] < most]
        mass, remaining = sum([loads[i] for i in candidates]), spare
        for i in candidates:
            addition = min(most - holding[i], max(1, remaining * loads[i] // mass), spare)
            holding[i] = holding[i] + addition
            spare = spare - addition
    return np.array(holding)


def noise(stream_key, extent, spread, limit, shards=(), kind=jnp.bfloat16):
    drawn = spread * jax.random.normal(stream_key, extent, jnp.float32)
    if shards:
        drawn = drawn * steps_of(stream_key, extent, shards, -0.22, 0.18)
    return jnp.clip(drawn, -limit, limit).astype(kind)


def setup_inputs(seed: int = 0) -> dict:
    streams_of = jax.random.split(jax.random.key(seed), 12)
    tokens = noise(streams_of[0], (SEQS, SEQLEN, D), 1.0, 6.0, ((0, 32), (1, 8)))
    route_keys = jax.random.split(jax.random.fold_in(streams_of[1], 1), SEQS * SEQLEN // TOK_DEV)
    route_turns = jax.random.permutation(jax.random.fold_in(streams_of[1], 3), SEQS * SEQLEN // TOK_DEV)
    route = jax.vmap(lambda own, number: routed_block(jax.random.fold_in(streams_of[1], 2), own, number, TOK_DEV, EXPERTS, 1, CAP, 1))(route_keys, route_turns).reshape((SEQS, SEQLEN, 1))
    w_inner = noise(streams_of[2], (EXPERTS, D, 2, DI), D ** -0.5, 0.125, ((0, 32), (3, 8)))
    w_state = noise(streams_of[3], (EXPERTS, D, 2 * NSTATE), (D * NSTATE) ** -0.5, 0.015625, ((0, 32),))
    w_step = noise(streams_of[4], (EXPERTS, D, HEADS), D ** -0.5, 0.125, ((0, 32), (2, 8)))
    step_bias = jnp.clip(-2.0 + 2.5 * jax.random.uniform(streams_of[5], (HEADS,), jnp.float32) ** steps_of(streams_of[5], (HEADS,), ((0, 8),), -0.2, 0.2), -2.0, 0.5)
    decay_log = jnp.clip(-7.0 + 4.5 * jax.random.uniform(streams_of[6], (HEADS,), jnp.float32) ** steps_of(streams_of[6], (HEADS,), ((0, 8),), -0.2, 0.2), -7.0, -2.5)
    skip_gain = jnp.clip(0.5 + 1.0 * jax.random.uniform(streams_of[7], (HEADS,), jnp.float32) ** steps_of(streams_of[7], (HEADS,), ((0, 8),), -0.2, 0.2), 0.5, 1.5)
    conv_weight = noise(streams_of[8], (CONV, DI), CONV ** -0.5, 3.0, ((1, 8),), jnp.float32)
    conv_bias = noise(streams_of[9], (DI,), 0.3, 1.5, ((0, 8),), jnp.float32)
    w_out = noise(streams_of[10], (EXPERTS, DI, D), DI ** -0.5, 0.09375, ((0, 32), (1, 8)))
    return {"tokens": tokens, "route": route, "w_inner": w_inner, "w_state": w_state, "w_step": w_step, "step_bias": step_bias, "decay_log": decay_log, "skip_gain": skip_gain, "conv_weight": conv_weight, "conv_bias": conv_bias, "w_out": w_out}


def block_ranks(ids_flat, experts, tok_rows):
    blocks = ids_flat.reshape(-1, tok_rows)
    onehot = (blocks[:, :, None] == jnp.arange(experts, dtype=jnp.int32)[None, None, :]).astype(jnp.int32)
    before = jnp.cumsum(onehot, axis=1) - 1
    return jnp.sum(onehot * before, axis=2).astype(jnp.int32)


def causal_conv(values, conv_weight, conv_bias):
    taps = conv_weight.shape[0]
    length = values.shape[0]
    padded = jnp.pad(values, ((taps - 1, 0), (0, 0)))
    total = conv_bias[None, :] + jnp.zeros_like(values)
    for shift in range(taps):
        total = total + conv_weight[shift][None, :] * padded[shift:shift + length]
    return total


def state_scan(signal_heads, steps, rates, in_vecs, out_vecs):
    length, heads, head_dim = signal_heads.shape
    nstate = in_vecs.shape[1]
    block = math.gcd(length, 128)
    count = length // block
    exact = lax.Precision.HIGHEST
    logs = steps * rates[None, :]
    pieces = (signal_heads.reshape(count, block, heads, head_dim), steps.reshape(count, block, heads),
              logs.reshape(count, block, heads), in_vecs.reshape(count, block, nstate),
              out_vecs.reshape(count, block, nstate))
    lower = jnp.arange(block)[:, None] >= jnp.arange(block)[None, :]

    def advance(state, piece):
        values, step_now, log_now, keys, queries = piece
        summed = jnp.cumsum(log_now, axis=0)
        gaps = summed[:, None, :] - summed[None, :, :]
        decay = jnp.exp(jnp.where(lower[:, :, None], gaps, -jnp.inf))
        scores = jnp.dot(queries, keys.T, precision=exact)
        weights = scores[:, :, None] * decay * step_now[None, :, :]
        local = jnp.einsum("tuh,uhp->thp", weights, values, precision=exact)
        carried = jnp.exp(summed)[:, :, None] * jnp.einsum("tn,hpn->thp", queries, state, precision=exact)
        tail = jnp.exp(summed[-1][None, :] - summed) * step_now
        state = jnp.exp(summed[-1])[:, None, None] * state + jnp.einsum("uh,uhp,un->hpn", tail, values, keys, precision=exact)
        return state, local + carried

    start = jnp.zeros((heads, head_dim, nstate), jnp.float32)
    final_state, outputs = lax.scan(advance, start, pieces)
    return outputs.reshape(length, heads, head_dim)


def mix_sequence(gate_inner, state_in_out, step_raw, conv_weight, conv_bias, step_bias, decay_log, skip_gain, head_dim):
    length = gate_inner.shape[0]
    gate_part = gate_inner[:, 0].astype(jnp.float32)
    inner_part = gate_inner[:, 1].astype(jnp.float32)
    signal = jax.nn.silu(causal_conv(inner_part, conv_weight, conv_bias))
    heads = step_raw.shape[1]
    steps = jax.nn.softplus(step_raw.astype(jnp.float32) + step_bias[None, :])
    rates = -jnp.exp(decay_log)
    nstate = state_in_out.shape[1] // 2
    in_vecs = state_in_out[:, :nstate].astype(jnp.float32)
    out_vecs = state_in_out[:, nstate:].astype(jnp.float32)
    signal_heads = signal.reshape(length, heads, head_dim)
    scanned = state_scan(signal_heads, steps, rates, in_vecs, out_vecs)
    scanned = scanned + skip_gain[None, :, None] * signal_heads
    return (scanned.reshape(length, heads * head_dim) * jax.nn.silu(gate_part)).astype(jnp.bfloat16)


def reference(tokens, route, w_inner, w_state, w_step, step_bias, decay_log, skip_gain, conv_weight, conv_bias, w_out):
    seqs, length, width = tokens.shape
    experts = w_inner.shape[0]
    inner = w_inner.shape[3]
    total = seqs * length
    ids = route.reshape(total).astype(jnp.int32)
    ranks = block_ranks(ids, experts, TOK_DEV).reshape(total)
    blocks_all = total // TOK_DEV
    block_of = jnp.arange(total, dtype=jnp.int32) // TOK_DEV
    slot = (ids * blocks_all + block_of) * CAP + ranks
    table = jnp.full((experts * blocks_all * CAP,), total, jnp.int32).at[slot].set(jnp.arange(total, dtype=jnp.int32))
    table = table.reshape(experts, blocks_all * CAP)
    flat = tokens.reshape(total, width)
    nboth = w_state.shape[2]
    heads = w_step.shape[2]

    def project(carry, item):
        rows_index, weight_inner, weight_state, weight_step = item
        rows = jnp.take(flat, rows_index, axis=0, mode="fill", fill_value=0)
        gate_inner = jnp.dot(rows, weight_inner.reshape(width, 2 * inner), preferred_element_type=jnp.float32).astype(jnp.bfloat16)
        state_part = jnp.dot(rows, weight_state, preferred_element_type=jnp.float32).astype(jnp.bfloat16)
        step_part = jnp.dot(rows, weight_step, preferred_element_type=jnp.float32).astype(jnp.bfloat16)
        return (carry[0].at[rows_index].set(gate_inner, mode="drop"),
                carry[1].at[rows_index].set(state_part, mode="drop"),
                carry[2].at[rows_index].set(step_part, mode="drop")), None

    start = (jnp.zeros((total, 2 * inner), jnp.bfloat16), jnp.zeros((total, nboth), jnp.bfloat16), jnp.zeros((total, heads), jnp.bfloat16))
    projected, unused = lax.scan(project, start, (table, w_inner, w_state, w_step))
    gate_all = projected[0].reshape(seqs, length, 2, inner)
    state_all = projected[1].reshape(seqs, length, nboth)
    step_all = projected[2].reshape(seqs, length, heads)

    def one_sequence(parts):
        return mix_sequence(parts[0], parts[1], parts[2], conv_weight, conv_bias, step_bias, decay_log, skip_gain, HEAD_DIM)

    gated = lax.map(one_sequence, (gate_all, state_all, step_all)).reshape(total, inner)
    group = inner // N_CONTEXT

    def output_rows(carry, item):
        rows_index, weight_out = item
        rows = jnp.take(gated, rows_index, axis=0, mode="fill", fill_value=0)
        summed = jnp.zeros((rows.shape[0], width), jnp.float32)
        for shard in range(N_CONTEXT):
            part = jnp.dot(rows[:, shard * group:(shard + 1) * group], weight_out[shard * group:(shard + 1) * group], preferred_element_type=jnp.float32).astype(jnp.bfloat16)
            summed = summed + lax.optimization_barrier(part).astype(jnp.float32)
        return carry.at[rows_index].set(summed.astype(jnp.bfloat16), mode="drop"), None

    result, unused_two = lax.scan(output_rows, jnp.zeros((total, width), jnp.bfloat16), (table, w_out))
    return result.reshape(seqs, length, width)
```

```python
import functools

import jax
import jax.numpy as jnp
from jax import lax
from jax.experimental import pallas as pl
from jax.experimental.pallas import tpu as pltpu
from jax.sharding import PartitionSpec as P

HEAD_DIM = 64
MESH = pl.DeviceIdType.MESH
F32 = jnp.float32
BF16 = jnp.bfloat16
VMEM_LIMIT = 60 * 1024 * 1024


def _dot(a, b, dims=((1,), (0,)), precision=None):
    return lax.dot_general(a, b, (dims, ((), ())), precision=precision, preferred_element_type=F32)


def _meet(expert_peers, context_peers):
    e, c = lax.axis_index("expert"), lax.axis_index("context")
    barrier = pltpu.get_barrier_semaphore()

    def greet(axis, me, count):
        def body(k, carry):
            peer = lax.rem(me + k, count)
            pl.semaphore_signal(barrier, inc=1, device_id={axis: peer}, device_id_type=MESH)
            return carry

        lax.fori_loop(1, count, body, 0)

    greet("expert", e, expert_peers)
    greet("context", c, context_peers)
    pl.semaphore_wait(barrier, expert_peers + context_peers - 2)


def _drain(ref, sem):
    pltpu.make_async_copy(ref, ref, sem).wait()


def _fold(top, bottom):
    n, w = top.shape[0] // 8, top.shape[1]
    return jnp.concatenate([top.reshape(n, 8, w), bottom.reshape(n, 8, w)], axis=1).astype(BF16)


def _unfold(folded):
    n, _, w = folded.shape
    wide = folded.astype(F32)
    return (
        wide[:, :8, :].reshape(n * 8, w).astype(BF16),
        wide[:, 8:, :].reshape(n * 8, w).astype(BF16),
    )


def _scatter_expert(E, src, dst, send_sem, recv_sem):
    e = lax.axis_index("expert")

    def body(k, carry):
        peer = lax.rem(e + k, E)
        pltpu.make_async_remote_copy(
            src_ref=src.at[peer],
            dst_ref=dst.at[e],
            send_sem=send_sem,
            recv_sem=recv_sem,
            device_id={"expert": peer},
            device_id_type=MESH,
        ).start()
        return carry

    lax.fori_loop(1, E, body, 0)
    dst[e] = src[e]


def _slot_onehot(row, n, half):
    place = row + (row & -8) + 8 * half
    return (lax.broadcasted_iota(jnp.int32, (n, row.shape[1]), 0) == place).astype(BF16)


def project_kernel(
    E,
    C,
    slots,
    tokens,
    w_inner_hbm,
    w_state,
    w_step,
    gate_out,
    inner_out,
    ss_out,
    w_inner,
    stok,
    rtok,
    rows,
    sinner,
    wstep_all,
    sss,
    rss,
    tok_sem,
    ss_sem,
    inner_send,
    inner_recv,
    row_send,
    row_recv,
    fwd_send,
    step_send,
    step_recv,
    pos_send,
    pos_recv,
    w_sem,
):
    e, c = lax.axis_index("expert"), lax.axis_index("context")
    x, core = c // 2, lax.rem(c, 2)
    sibling = c + 1 - 2 * core
    chips = C // 2
    width = tokens.shape[1]
    half = width // 2
    chans = inner_out.shape[3]
    nrow = E * 8

    load_w = pltpu.make_async_copy(w_inner_hbm, w_inner, w_sem)
    load_w.start()

    row = slots[pl.ds(c, 1), :]
    dispatch = (lax.broadcasted_iota(jnp.int32, (nrow, row.shape[1]), 0) == row).astype(BF16)
    for part in range(2):
        cols = slice(part * half // 2, (part + 1) * half // 2)
        late = slice(half + part * half // 2, half + (part + 1) * half // 2)
        stok[:, :, cols] = _fold(_dot(dispatch, tokens[:, cols]), _dot(dispatch, tokens[:, late]))
    heads = w_step.shape[0]
    wide = w_step[...].astype(F32)
    wstep_all[c] = jnp.concatenate([wide, jnp.zeros((16 - heads, width), F32)], axis=0).astype(BF16)

    _meet(E, C)
    _scatter_expert(E, stok, rtok, tok_sem.at[0], tok_sem.at[1])

    def share(ref, send_sem, recv_sem):
        def body(k, carry):
            peer = lax.rem(c + k, C)
            pltpu.make_async_remote_copy(
                src_ref=ref.at[c],
                dst_ref=ref.at[c],
                send_sem=send_sem,
                recv_sem=recv_sem,
                device_id={"context": peer},
                device_id_type=MESH,
            ).start()
            return carry

        lax.fori_loop(1, C, body, 0)

    share(wstep_all, step_send, step_recv)

    _drain(rtok.at[pl.ds(0, E - 1)], tok_sem.at[1])
    for part in range(2):
        cols = slice(part * half // 2, (part + 1) * half // 2)
        late = slice(half + part * half // 2, half + (part + 1) * half // 2)
        left, right = _unfold(rtok[:, :, cols])
        rows[c, :, cols] = left
        rows[c, :, late] = right

    def send_rows(block, target, send_sem):
        return pltpu.make_async_remote_copy(
            src_ref=rows.at[block],
            dst_ref=rows.at[block],
            send_sem=send_sem,
            recv_sem=row_recv.at[block],
            device_id={"context": target},
            device_id_type=MESH,
        )

    for k in range(1, chips):
        send_rows(c, lax.rem(x + k, chips) * 2 + core, row_send.at[k]).start()
    send_rows(c, sibling, row_send.at[0]).start()

    _drain(wstep_all.at[pl.ds(0, C - 1)], step_recv)
    state = _dot(rows[c], w_state[...])
    step = _dot(rows[c], wstep_all[...].reshape(C * 16, width), ((1,), (1,)))
    both = jnp.concatenate([state, step], axis=1)
    sss[...] = _fold(both, jnp.zeros_like(both))
    _scatter_expert(E, sss, rss, ss_sem.at[0], ss_sem.at[1])

    def project(chip):
        pair = rows[pl.ds(chip * 2, 2)].reshape(2 * nrow, width)
        step_n = min(256, chans)
        for n in range(chans // step_n):
            cols = slice(n * step_n, (n + 1) * step_n)
            there = slice(chans + n * step_n, chans + (n + 1) * step_n)
            res = _dot(pair, w_inner[:, there])
            sinner[chip, :, :, cols] = _fold(res[:nrow], res[nrow:])
        _scatter_expert(E, sinner.at[chip], inner_out.at[chip], inner_send.at[chip], inner_recv.at[chip])
        for n in range(chans // step_n):
            cols = slice(n * step_n, (n + 1) * step_n)
            res = _dot(pair, w_inner[:, cols])
            gate_out[chip, :, :, cols] = _fold(res[:nrow], res[nrow:])

    load_w.wait()
    _drain(rows.at[0], row_recv.at[sibling])
    project(x)

    _drain(rss.at[pl.ds(0, E - 1)], ss_sem.at[1])
    here = _slot_onehot(row, E * 16, 0)
    ss_out[c] = _dot(here, rss[...].reshape(E * 16, rss.shape[2]), ((0,), (0,))).astype(BF16)
    share(ss_out, pos_send, pos_recv)

    def remote_chip(i, carry):
        far = 1 + 2 * i - 3 * (i // 2)
        chip = lax.rem(x + far, chips)
        block = chip * 2 + core
        _drain(rows.at[0], row_recv.at[block])
        send_rows(block, sibling, fwd_send.at[i]).start()
        _drain(rows.at[0], row_recv.at[chip * 2 + 1 - core])
        project(chip)
        return carry

    lax.fori_loop(0, chips - 1, remote_chip, 0)

    _drain(ss_out.at[pl.ds(0, C - 1)], pos_recv)
    for chip in range(chips):
        _drain(inner_out.at[chip, pl.ds(0, E - 1)], inner_recv.at[chip])
    _drain(stok.at[pl.ds(0, E - 1)], tok_sem.at[0])
    _drain(sss.at[pl.ds(0, E - 1)], ss_sem.at[0])
    _drain(wstep_all.at[pl.ds(0, C - 1)], step_send)
    _drain(ss_out.at[pl.ds(0, C - 1)], pos_send)
    for chip in range(chips):
        _drain(sinner.at[chip, pl.ds(0, E - 1)], inner_send.at[chip])
        _drain(rows.at[0], row_send.at[chip])
        if chip < chips - 1:
            _drain(rows.at[0], fwd_send.at[chip])


def scan_kernel(
    E,
    C,
    slots,
    inner,
    ss,
    conv_weight,
    conv_bias,
    per_lane,
    per_row,
    skip,
    back_out,
    state,
    tail8,
    scanned,
    sback,
    send_sem,
    recv_sem,
):
    c = lax.axis_index("context")
    exact = lax.Precision.HIGHEST
    T = slots.shape[1]
    chans = inner.shape[3]
    heads = chans // HEAD_DIM
    taps = conv_weight.shape[0]
    nbc = HEAD_DIM

    _meet(E, 1)

    state[...] = jnp.zeros_like(state)
    tail8[...] = jnp.zeros_like(tail8)
    at0 = lax.broadcasted_iota(jnp.int32, (T, T), 0)
    at1 = lax.broadcasted_iota(jnp.int32, (T, T), 1)
    lower = at0 >= at1
    lower_one = lower.astype(F32)
    upper_one = (at0 <= at1).astype(F32)
    lane = lax.broadcasted_iota(jnp.int32, (T, 2 * HEAD_DIM), 1)
    first = lane < HEAD_DIM
    lanes = C * 16
    pick = (
        lax.broadcasted_iota(jnp.int32, (lanes, 128), 0)
        == c * 16 + lax.broadcasted_iota(jnp.int32, (lanes, 128), 1)
    ) & (lax.broadcasted_iota(jnp.int32, (lanes, 128), 1) < heads)
    pick = pick.astype(BF16)
    pick_t = (
        lax.broadcasted_iota(jnp.int32, (16, lanes), 1)
        == c * 16 + lax.broadcasted_iota(jnp.int32, (16, lanes), 0)
    ).astype(BF16)
    bias_l, rate_l = per_lane[0:1, :], -jnp.exp(per_lane[1:2, :])
    bias_r, rate_r = per_row[:, 0:1], -jnp.exp(per_row[:, 1:2])

    def softplus(v):
        return jnp.maximum(v, 0.0) + jnp.log1p(jnp.exp(-jnp.abs(v)))

    def chunk(b, half):
        bp = b // 2
        row = slots[pl.ds(b, 1), :]
        place = _slot_onehot(row, E * 16, half)
        raw = _dot(place, inner[bp].reshape(E * 16, chans), ((0,), (0,)))
        joined = jnp.concatenate([tail8[...], raw], axis=0)
        tail8[...] = raw[T - 8 :, :]
        conv = conv_bias[...] + jnp.zeros_like(raw)
        for j in range(taps):
            begin = 8 - taps + 1 + j
            conv = conv + conv_weight[j : j + 1, :] * joined[begin : begin + T, :]
        signal = conv * jax.nn.sigmoid(conv)

        mine = ss[b]
        keys, queries = mine[:, :nbc], mine[:, nbc : 2 * nbc]
        raw_step = mine[:, 2 * nbc :]
        steps = softplus(_dot(raw_step, pick) + bias_l)
        steps_t = softplus(_dot(pick_t, raw_step, ((1,), (1,))) + bias_r)
        summed = _dot(lower_one, steps * rate_l, precision=exact)
        summed_t = _dot(steps_t * rate_r, upper_one, precision=exact)
        scores = _dot(queries, keys, ((1,), (1,)))
        grown = jnp.exp(summed)
        end = summed[T - 1 : T, :]
        tail = jnp.exp(end - summed) * steps
        whole = jnp.exp(end)
        for pair in range(heads // 2):
            cols = slice(pair * 2 * HEAD_DIM, (pair + 1) * 2 * HEAD_DIM)
            xs = signal[:, cols]
            xb = xs.astype(BF16)
            weights = []
            for h in (2 * pair, 2 * pair + 1):
                gaps = summed[:, h : h + 1] - summed_t[h : h + 1, :]
                decay = jnp.exp(jnp.where(lower, gaps, -jnp.inf))
                weights.append((scores * decay * steps_t[h : h + 1, :]).astype(BF16))
            zero = jnp.zeros_like(xb)
            stacked = jnp.concatenate([jnp.where(first, xb, zero), jnp.where(first, zero, xb)], axis=0)
            local = _dot(jnp.concatenate(weights, axis=1), stacked)

            def spread(v, n):
                a = jnp.broadcast_to(v[:, 2 * pair : 2 * pair + 1], (n, 2 * HEAD_DIM))
                z = jnp.broadcast_to(v[:, 2 * pair + 1 : 2 * pair + 2], (n, 2 * HEAD_DIM))
                return jnp.where(first[:n], a, z)

            old = state[:, cols]
            carried = spread(grown, T) * _dot(queries, old.astype(BF16))
            fed = (spread(tail, T) * xs).astype(BF16)
            state[:, cols] = spread(whole, 1) * old + _dot(keys, fed, ((0,), (0,)))
            scanned[half, :, cols] = (local + carried + skip[:, cols] * xs).astype(BF16)

    def pair_of_chunks(bp, carry):
        chunk(2 * bp, 0)
        chunk(2 * bp + 1, 1)
        total = None
        for half in range(2):
            row = slots[pl.ds(2 * bp + half, 1), :]
            term = _dot(_slot_onehot(row, E * 16, half), scanned[half])
            total = term if total is None else total + term
        sback[bp] = total.astype(BF16).reshape(E, 16, chans)
        _scatter_expert(E, sback.at[bp], back_out.at[bp], send_sem.at[bp], recv_sem.at[bp])
        return carry

    lax.fori_loop(0, C // 2, pair_of_chunks, 0)
    for chip in range(C // 2):
        _drain(back_out.at[chip, pl.ds(0, E - 1)], recv_sem.at[chip])
    for chip in range(C // 2):
        _drain(sback.at[chip, pl.ds(0, E - 1)], send_sem.at[chip])


def mix_kernel(
    E,
    C,
    slots,
    back,
    gate,
    w_out_hbm,
    out,
    w_out,
    gated,
    kept,
    sib_src,
    sib_dst,
    far_src,
    far_dst,
    fin_src,
    fin_dst,
    sib_send,
    sib_recv,
    far_send,
    far_recv,
    fin_send,
    fin_recv,
    w_sem,
):
    c = lax.axis_index("context")
    x, core = c // 2, lax.rem(c, 2)
    sibling = c + 1 - 2 * core
    chips = C // 2
    nrow = E * 8
    parts, _, _, step_n = kept.shape
    chans = back.shape[3]

    load_w = pltpu.make_async_copy(w_out_hbm, w_out, w_sem)
    load_w.start()
    for chip in range(chips):
        g = gate[chip].astype(F32)
        v = back[chip].astype(F32) * (g * jax.nn.sigmoid(g))
        gated[chip] = v.astype(BF16)
    _meet(E, C)
    load_w.wait()

    for j in range(parts):

        def emit(chip, carry):
            rows = gated[chip].reshape(2 * nrow, chans)
            part = _dot(rows, w_out[:, j * step_n : (j + 1) * step_n])
            part = part.reshape(E, 2, 8, step_n)
            both = jnp.stack([part[:, 0].reshape(nrow, step_n), part[:, 1].reshape(nrow, step_n)])
            kept[j, chip] = jnp.where(core == 0, both[0], both[1]).astype(BF16)
            sib_src[j, chip] = jnp.where(core == 0, both[1], both[0]).astype(BF16)
            return carry

        lax.fori_loop(0, chips, emit, 0)
        pltpu.make_async_remote_copy(
            src_ref=sib_src.at[j],
            dst_ref=sib_dst.at[j],
            send_sem=sib_send.at[j],
            recv_sem=sib_recv.at[j],
            device_id={"context": sibling},
            device_id_type=MESH,
        ).start()

    def far_copy(j, k):
        chip = lax.rem(x + k, chips)
        return pltpu.make_async_remote_copy(
            src_ref=far_src.at[j, k - 1],
            dst_ref=far_dst.at[j, k - 1],
            send_sem=far_send.at[j, k - 1],
            recv_sem=far_recv.at[j, k - 1],
            device_id={"context": chip * 2 + core},
            device_id_type=MESH,
        )

    for j in range(parts):
        _drain(sib_dst.at[j], sib_recv.at[j])

        def forward(k, carry):
            chip = lax.rem(x + k, chips)
            both = kept[j, chip].astype(F32) + sib_dst[j, chip].astype(F32)
            far_src[j, k - 1] = both.astype(BF16)
            far_copy(j, k).start()
            return carry

        lax.fori_loop(1, chips, forward, 0)

    for j in range(parts):
        total = kept[j, x].astype(F32) + sib_dst[j, x].astype(F32)
        for k in range(1, chips):
            _drain(far_dst.at[j, k - 1], far_recv.at[j, k - 1])
            total = total + far_dst[j, k - 1].astype(F32)
        fin_src[j] = _fold(total[:, : step_n // 2], total[:, step_n // 2 :])
        _scatter_expert(E, fin_src.at[j], fin_dst.at[j], fin_send.at[j], fin_recv.at[j])

    row = slots[pl.ds(c, 1), :]
    places = [_slot_onehot(row, E * 16, half) for half in range(2)]
    for j in range(parts):
        _drain(fin_dst.at[j, pl.ds(0, E - 1)], fin_recv.at[j])
        arrived = fin_dst[j].reshape(E * 16, step_n // 2)
        for half in range(2):
            begin = j * step_n + half * (step_n // 2)
            res = _dot(places[half], arrived, ((0,), (0,)))
            out[:, begin : begin + step_n // 2] = res.astype(BF16)

    for j in range(parts):
        _drain(sib_src.at[j], sib_send.at[j])
        _drain(fin_src.at[j, pl.ds(0, E - 1)], fin_send.at[j])
        for k in range(1, chips):
            _drain(far_src.at[j, k - 1], far_send.at[j, k - 1])


def per_device(
    tokens,
    route,
    w_inner,
    w_state,
    w_step,
    step_bias,
    decay_log,
    skip_gain,
    conv_weight,
    conv_bias,
    w_out,
):
    T, width = tokens.shape[1:]
    E, C = lax.axis_size("expert"), lax.axis_size("context")
    chips = C // 2
    chans = w_inner.shape[3]
    heads = w_step.shape[2]
    nboth = w_state.shape[2]
    ids = route[0, :, 0].reshape(C, T)
    same = ids[:, :, None] == ids[:, None, :]
    before = jnp.arange(T)[None, :] < jnp.arange(T)[:, None]
    ranks = jnp.sum((same & before[None]).astype(jnp.int32), axis=2)
    slots = ids * 8 + ranks

    vmem = pl.BlockSpec(memory_space=pltpu.VMEM)
    hbm = pl.BlockSpec(memory_space=pl.ANY)
    dma = pltpu.SemaphoreType.DMA
    flat = jax.ShapeDtypeStruct((chips, E, 16, chans), BF16)

    def params(number):
        return pltpu.CompilerParams(
            collective_id=number, has_side_effects=True, vmem_limit_bytes=VMEM_LIMIT
        )

    wide = nboth + C * 16
    gate, inner, ss = pl.pallas_call(
        functools.partial(project_kernel, E, C),
        out_shape=(flat, flat, jax.ShapeDtypeStruct((C, T, wide), BF16)),
        in_specs=[vmem, vmem, hbm, vmem, vmem],
        out_specs=(vmem, vmem, vmem),
        scratch_shapes=[
            pltpu.VMEM((width, 2 * chans), BF16),
            pltpu.VMEM((E, 16, width // 2), BF16),
            pltpu.VMEM((E, 16, width // 2), BF16),
            pltpu.VMEM((C, E * 8, width), BF16),
            pltpu.VMEM((chips, E, 16, chans), BF16),
            pltpu.VMEM((C, 16, width), BF16),
            pltpu.VMEM((E, 16, wide), BF16),
            pltpu.VMEM((E, 16, wide), BF16),
            dma((2,)),
            dma((2,)),
            dma((chips,)),
            dma((chips,)),
            dma((chips,)),
            dma((C,)),
            dma((chips,)),
            dma,
            dma,
            dma,
            dma,
            dma,
        ],
        compiler_params=params(0),
        name="project",
    )(slots, tokens[0], w_inner[0].reshape(width, 2 * chans), w_state[0], w_step[0].T)

    pad = 128 - heads
    per_lane = jnp.pad(jnp.stack([step_bias, decay_log]), ((0, 0), (0, pad)))
    per_row = jnp.pad(jnp.stack([step_bias, decay_log], axis=1), ((0, 16 - heads), (0, 0)))
    back = pl.pallas_call(
        functools.partial(scan_kernel, E, C),
        out_shape=flat,
        in_specs=[vmem] * 8,
        out_specs=vmem,
        scratch_shapes=[
            pltpu.VMEM((HEAD_DIM, chans), F32),
            pltpu.VMEM((8, chans), F32),
            pltpu.VMEM((2, T, chans), BF16),
            pltpu.VMEM((chips, E, 16, chans), BF16),
            dma((chips,)),
            dma((chips,)),
        ],
        compiler_params=params(1),
        name="scan",
    )(
        slots,
        inner,
        ss,
        conv_weight,
        conv_bias[None, :],
        per_lane,
        per_row,
        jnp.repeat(skip_gain, HEAD_DIM)[None, :],
    )

    parts = 4
    step_n = width // parts
    blocks = (parts, chips, E * 8, step_n)
    fars = (parts, chips - 1, E * 8, step_n)
    fins = (parts, E, 16, step_n // 2)
    mixed = pl.pallas_call(
        functools.partial(mix_kernel, E, C),
        out_shape=jax.ShapeDtypeStruct((T, width), BF16),
        in_specs=[vmem, vmem, vmem, hbm],
        out_specs=vmem,
        scratch_shapes=[
            pltpu.VMEM((chans, width), BF16),
            pltpu.VMEM((chips, E, 16, chans), BF16),
            pltpu.VMEM(blocks, BF16),
            pltpu.VMEM(blocks, BF16),
            pltpu.VMEM(blocks, BF16),
            pltpu.VMEM(fars, BF16),
            pltpu.VMEM(fars, BF16),
            pltpu.VMEM(fins, BF16),
            pltpu.VMEM(fins, BF16),
            dma((parts,)),
            dma((parts,)),
            dma((parts, chips - 1)),
            dma((parts, chips - 1)),
            dma((parts,)),
            dma((parts,)),
            dma,
        ],
        compiler_params=params(2),
        name="mix",
    )(slots, back, gate, w_out[0])
    return mixed[None]


def solution(mesh):
    in_specs = (
        P("expert", "context", None),
        P("expert", None, None),
        P("expert", None, None, "context"),
        P("expert", None, None),
        P("expert", None, "context"),
        P("context"),
        P("context"),
        P("context"),
        P(None, "context"),
        P("context"),
        P("expert", "context", None),
    )
    out_specs = P("expert", "context", None)
    return jax.shard_map(
        per_device, mesh=mesh, in_specs=in_specs, out_specs=out_specs, check_vma=False
    )
```

```python
import functools

import jax
import jax.numpy as jnp
from jax import lax
from jax.experimental import pallas as pl
from jax.experimental.pallas import tpu as pltpu
from jax.sharding import PartitionSpec as P

HEAD_DIM = 64
MESH = pl.DeviceIdType.MESH
F32 = jnp.float32
BF16 = jnp.bfloat16
VMEM_LIMIT = 60 * 1024 * 1024


def _dot(a, b, dims=((1,), (0,)), precision=None):
    return lax.dot_general(a, b, (dims, ((), ())), precision=precision, preferred_element_type=F32)


def _meet(expert_peers, context_peers):
    e, c = lax.axis_index("expert"), lax.axis_index("context")
    barrier = pltpu.get_barrier_semaphore()

    def greet(axis, me, count):
        def body(k, carry):
            peer = lax.rem(me + k, count)
            pl.semaphore_signal(barrier, inc=1, device_id={axis: peer}, device_id_type=MESH)
            return carry

        lax.fori_loop(1, count, body, 0)

    greet("expert", e, expert_peers)
    greet("context", c, context_peers)
    pl.semaphore_wait(barrier, expert_peers + context_peers - 2)


def _drain(ref, sem):
    pltpu.make_async_copy(ref, ref, sem).wait()


def _fold(top, bottom):
    n, w = top.shape[0] // 8, top.shape[1]
    return jnp.concatenate([top.reshape(n, 8, w), bottom.reshape(n, 8, w)], axis=1).astype(BF16)


def _unfold(folded):
    n, _, w = folded.shape
    wide = folded.astype(F32)
    return (
        wide[:, :8, :].reshape(n * 8, w).astype(BF16),
        wide[:, 8:, :].reshape(n * 8, w).astype(BF16),
    )


def _scatter_expert(E, src, dst, send_sem, recv_sem):
    e = lax.axis_index("expert")

    def body(k, carry):
        peer = lax.rem(e + k, E)
        pltpu.make_async_remote_copy(
            src_ref=src.at[peer],
            dst_ref=dst.at[e],
            send_sem=send_sem,
            recv_sem=recv_sem,
            device_id={"expert": peer},
            device_id_type=MESH,
        ).start()
        return carry

    lax.fori_loop(1, E, body, 0)
    dst[e] = src[e]


def _slot_onehot(row, n, half):
    place = row + (row & -8) + 8 * half
    return (lax.broadcasted_iota(jnp.int32, (n, row.shape[1]), 0) == place).astype(BF16)


def _remote(src, dst, send_sem, recv_sem, **where):
    return pltpu.make_async_remote_copy(
        src_ref=src,
        dst_ref=dst,
        send_sem=send_sem,
        recv_sem=recv_sem,
        device_id=where,
        device_id_type=MESH,
    )


def _softplus(v):
    return jnp.maximum(v, 0.0) + jnp.log1p(jnp.exp(-jnp.abs(v)))


def _iota(shape, axis):
    return lax.broadcasted_iota(jnp.int32, shape, axis)


def layer_kernel(
    E,
    C,
    ids,
    tokens,
    w_inner_hbm,
    w_state,
    w_step,
    step_bias,
    decay_log,
    skip_gain,
    conv_weight,
    conv_bias,
    w_out_hbm,
    out,
    slots,
    w3,
    w_inner,
    w_out,
    stok,
    rtok,
    rows,
    sinner,
    inner,
    gate,
    sback,
    back,
    wstep_all,
    sss,
    rss,
    ss,
    gathered,
    fin_src,
    fin_dst,
    state,
    tail8,
    scanned,
    w3_sem,
    w_sem,
    tok_send,
    tok_recv,
    step_send,
    step_recv,
    row_send,
    row_recv,
    fwd_send,
    hop_send,
    ss_send,
    ss_recv,
    pos_send,
    pos_recv,
    inner_send,
    inner_recv,
    wout_send,
    wout_recv,
    back_send,
    back_recv,
    gated_send,
    gated_recv,
    fin_send,
    fin_recv,
):
    e, c = lax.axis_index("expert"), lax.axis_index("context")
    x, core = c // 2, lax.rem(c, 2)
    sibling = c + 1 - 2 * core
    chips = C // 2
    T, width = tokens.shape
    half = width // 2
    quarter = width // 4
    chans = inner.shape[3]
    nrow = E * 8
    nslot = E * 16
    heads = w_step.shape[0]
    pieces, piece = w3.shape[0], w3.shape[1]
    count = width // piece
    early = w_out.shape[1] // 8
    peers = pl.ds(0, E - 1)

    def load_piece(q):
        return pltpu.make_async_copy(
            w_inner_hbm.at[pl.ds(q * piece, piece)], w3.at[q % pieces], w3_sem.at[q % pieces]
        )

    for q in range(pieces):
        load_piece(q).start()
    load_w_out = pltpu.make_async_copy(w_out_hbm, w_out.at[c], w_sem)
    load_w_out.start()

    values = ids[...].astype(F32)
    eye = (_iota((T, T), 0) == _iota((T, T), 1)).astype(BF16)
    columns = _dot(eye, values.astype(BF16), ((1,), (1,)))
    earlier = _iota((T, T), 0) < _iota((T, T), 1)
    for b in range(C):
        same = (columns[:, b : b + 1] == values[b : b + 1, :]) & earlier
        rank = jnp.sum(same.astype(F32), axis=0, keepdims=True)
        slots[b : b + 1, :] = ids[b : b + 1, :] * 8 + rank.astype(jnp.int32)

    row = slots[pl.ds(c, 1), :]
    dispatch = (_iota((nrow, T), 0) == row).astype(BF16)

    def pack(h):
        a = h * half
        stok[h] = _fold(
            _dot(dispatch, tokens[:, a : a + quarter]),
            _dot(dispatch, tokens[:, a + quarter : a + half]),
        )

    pack(0)
    _meet(E, C)
    _scatter_expert(E, stok.at[0], rtok.at[0], tok_send.at[0], tok_recv.at[0])
    pack(1)
    _scatter_expert(E, stok.at[1], rtok.at[1], tok_send.at[1], tok_recv.at[1])

    def share(ref, send_sem, recv_sem):
        def body(k, carry):
            peer = lax.rem(c + k, C)
            _remote(ref.at[c], ref.at[c], send_sem, recv_sem, context=peer).start()
            return carry

        lax.fori_loop(1, C, body, 0)

    wide = w_step[...].astype(F32)
    wstep_all[c] = jnp.concatenate([wide, jnp.zeros((16 - heads, width), F32)], axis=0).astype(BF16)
    share(wstep_all, step_send, step_recv)

    def send_w_out(k, part):
        where = pl.ds(0, early) if part == 0 else pl.ds(early, w_out.shape[1] - early)
        return _remote(
            w_out.at[c, where],
            w_out.at[c, where],
            wout_send.at[part, k],
            wout_recv.at[part, c],
            context=lax.rem(x + k, chips) * 2 + core,
        )

    load_w_out.wait()
    for k in range(1, chips):
        send_w_out(k, 0).start()

    for q in range(count):
        load_piece(q).wait()

        def part_w(i, carry):
            block = w3[q % pieces, pl.ds(i * 128, 128)]
            at = pl.ds(pl.multiple_of(q * piece + i * 128, 128), 128)
            w_inner[0, at, :] = block[:, 0, :]
            w_inner[1, at, :] = block[:, 1, :]
            return carry

        lax.fori_loop(0, piece // 128, part_w, 0)
        if q + pieces < count:
            load_piece(q + pieces).start()

    right = lax.rem(x + 1, chips) * 2 + core
    left = lax.rem(x + chips - 1, chips) * 2 + core
    across = lax.rem(x + chips // 2, chips) * 2 + core

    def send_rows(h, block, target, sem):
        return _remote(rows.at[h, block], rows.at[h, block], sem, row_recv.at[h, block], context=target)

    def await_rows(h, block):
        _drain(rows.at[h, block], row_recv.at[h, block])

    for h in range(2):
        _drain(rtok.at[h, peers], tok_recv.at[h])
        first_q, second_q = _unfold(rtok[h])
        rows[h, c, :, :quarter] = first_q
        rows[h, c, :, quarter:] = second_q
        send_rows(h, c, right, row_send.at[h, 0]).start()
        send_rows(h, c, left, row_send.at[h, 1]).start()
        send_rows(h, c, sibling, row_send.at[h, 2]).start()

    _drain(wstep_all.at[pl.ds(0, C - 1)], step_recv)
    both = []
    for h in range(2):
        mine = rows[h, c]
        at = slice(h * half, (h + 1) * half)
        step_w = wstep_all[:, :, at].reshape(C * 16, half)
        both.append(
            jnp.concatenate([_dot(mine, w_state[at, :]), _dot(mine, step_w, ((1,), (1,)))], axis=1)
        )
    vectors = both[0] + both[1]
    sss[...] = _fold(vectors, jnp.zeros_like(vectors))
    _scatter_expert(E, sss, rss, ss_send, ss_recv)

    step_n = min(256, chans)

    def project(chip, which, dst):
        first = rows[0, pl.ds(chip * 2, 2)].reshape(2 * nrow, half)
        second = rows[1, pl.ds(chip * 2, 2)].reshape(2 * nrow, half)
        for n in range(chans // step_n):
            cols = slice(n * step_n, (n + 1) * step_n)
            res = _dot(first, w_inner[which, :half, cols]) + _dot(second, w_inner[which, half:, cols])
            dst[chip, :, :, cols] = _fold(res[:nrow], res[nrow:])

    def inner_chip(i, carry):
        chip = lax.rem(x + i + i // 2 - 2 * (i // 3), chips)

        @pl.when(i == 1)
        def _():
            await_rows(0, left)
            send_rows(0, left, right, hop_send.at[0]).start()
            send_rows(0, left, sibling, fwd_send.at[0, 0]).start()
            await_rows(0, right)
            send_rows(0, right, sibling, fwd_send.at[0, 1]).start()
            await_rows(1, right)
            send_rows(1, right, left, hop_send.at[1]).start()
            send_rows(1, right, sibling, fwd_send.at[1, 1]).start()
            await_rows(1, left)
            send_rows(1, left, sibling, fwd_send.at[1, 0]).start()

        @pl.when(i == chips - 1)
        def _():
            for h in range(2):
                await_rows(h, across)
                send_rows(h, across, sibling, fwd_send.at[h, 2]).start()

        for h in range(2):
            await_rows(h, chip * 2 + 1 - core)
        project(chip, 1, sinner)
        _scatter_expert(E, sinner.at[chip], inner.at[chip], inner_send.at[chip], inner_recv.at[chip])
        return carry

    lax.fori_loop(0, chips, inner_chip, 0)

    _remote(w_out.at[c], w_out.at[c], wout_send.at[0, 0], wout_recv.at[2, c], context=sibling).start()
    send_w_out(1, 1).start()
    send_w_out(chips - 1, 1).start()

    _drain(rss.at[peers], ss_recv)
    here = _slot_onehot(row, nslot, 0)
    ss[c] = _dot(here, rss[...].reshape(nslot, rss.shape[2]), ((0,), (0,))).astype(BF16)
    share(ss, pos_send, pos_recv)

    def gate_chip(chip, carry):
        project(chip, 0, gate)
        return carry

    lax.fori_loop(0, chips, gate_chip, 0)

    exact = lax.Precision.HIGHEST
    taps = conv_weight.shape[0]
    nbc = HEAD_DIM
    state[...] = jnp.zeros_like(state)
    tail8[...] = jnp.zeros_like(tail8)
    lower = _iota((T, T), 0) >= _iota((T, T), 1)
    lower_one = lower.astype(F32)
    upper_one = (_iota((T, T), 0) <= _iota((T, T), 1)).astype(F32)
    first = _iota((T, 2 * HEAD_DIM), 1) < HEAD_DIM
    lanes = C * 16
    pick = (_iota((lanes, heads), 0) == c * 16 + _iota((lanes, heads), 1)).astype(BF16)
    pick_t = (_iota((heads, lanes), 1) == c * 16 + _iota((heads, lanes), 0)).astype(BF16)
    diagonal = _iota((heads, heads), 0) == _iota((heads, heads), 1)

    def column(v):
        return jnp.sum(jnp.where(diagonal, v, 0.0), axis=1, keepdims=True)

    bias_l, rate_l = step_bias[...], -jnp.exp(decay_log[...])
    bias_r, rate_r = column(bias_l), column(rate_l)
    gain = skip_gain[...]

    def chunk(b, part):
        place = _slot_onehot(slots[pl.ds(b, 1), :], nslot, part)
        raw = _dot(place, inner[b // 2].reshape(nslot, chans), ((0,), (0,)))
        joined = jnp.concatenate([tail8[...], raw], axis=0)
        tail8[...] = raw[T - 8 :, :]
        conv = conv_bias[...] + jnp.zeros_like(raw)
        for j in range(taps):
            begin = 8 - taps + 1 + j
            conv = conv + conv_weight[j : j + 1, :] * joined[begin : begin + T, :]
        signal = conv * jax.nn.sigmoid(conv)

        mine = ss[b]
        keys, queries = mine[:, :nbc], mine[:, nbc : 2 * nbc]
        raw_step = mine[:, 2 * nbc :]
        steps = _softplus(_dot(raw_step, pick) + bias_l)
        steps_t = _softplus(_dot(pick_t, raw_step, ((1,), (1,))) + bias_r)
        summed = _dot(lower_one, steps * rate_l, precision=exact)
        summed_t = _dot(steps_t * rate_r, upper_one, precision=exact)
        scores = _dot(queries, keys, ((1,), (1,)))
        grown = jnp.exp(summed)
        end = summed[T - 1 : T, :]
        tail = jnp.exp(end - summed) * steps
        whole = jnp.exp(end)
        for pair in range(heads // 2):
            cols = slice(pair * 2 * HEAD_DIM, (pair + 1) * 2 * HEAD_DIM)
            xs = signal[:, cols]
            xb = xs.astype(BF16)
            weights = []
            for h in (2 * pair, 2 * pair + 1):
                gaps = summed[:, h : h + 1] - summed_t[h : h + 1, :]
                decay = jnp.exp(jnp.where(lower, gaps, -jnp.inf))
                weights.append((scores * decay * steps_t[h : h + 1, :]).astype(BF16))
            zero = jnp.zeros_like(xb)
            stacked = jnp.concatenate([jnp.where(first, xb, zero), jnp.where(first, zero, xb)], axis=0)
            local = _dot(jnp.concatenate(weights, axis=1), stacked)

            def spread(v):
                n = v.shape[0]
                a = jnp.broadcast_to(v[:, 2 * pair : 2 * pair + 1], (n, 2 * HEAD_DIM))
                z = jnp.broadcast_to(v[:, 2 * pair + 1 : 2 * pair + 2], (n, 2 * HEAD_DIM))
                return jnp.where(first[:n], a, z)

            old = state[:, cols]
            carried = spread(grown) * _dot(queries, old.astype(BF16))
            fed = (spread(tail) * xs).astype(BF16)
            state[:, cols] = spread(whole) * old + _dot(keys, fed, ((0,), (0,)))
            scanned[part, :, cols] = (local + carried + spread(gain) * xs).astype(BF16)

    _drain(ss.at[pl.ds(0, C - 1)], pos_recv)

    def pair_of_chunks(bp, carry):
        _drain(inner.at[bp, peers], inner_recv.at[bp])
        chunk(2 * bp, 0)
        chunk(2 * bp + 1, 1)
        total = None
        for part in range(2):
            place = _slot_onehot(slots[pl.ds(2 * bp + part, 1), :], nslot, part)
            term = _dot(place, scanned[part])
            total = term if total is None else total + term
        sback[bp] = total.astype(BF16).reshape(E, 16, chans)
        _scatter_expert(E, sback.at[bp], back.at[bp], back_send.at[bp], back_recv.at[bp])

        @pl.when(bp == 1)
        def _():
            send_w_out(2, 1).start()

        return carry

    lax.fori_loop(0, chips, pair_of_chunks, 0)

    def forward_w_out(block, k):
        pltpu.make_async_copy(
            w_out.at[block, pl.ds(0, early)], w_out.at[block, pl.ds(0, early)], wout_recv.at[0, block]
        ).wait()
        rest = pl.ds(early, w_out.shape[1] - early)
        pltpu.make_async_copy(
            w_out.at[block, rest], w_out.at[block, rest], wout_recv.at[1, block]
        ).wait()
        _remote(
            w_out.at[block], w_out.at[block], wout_send.at[1, 0] if k == 0 else fwd_send.at[k - 1, 3],
            wout_recv.at[2, block], context=sibling,
        ).start()

    forward_w_out(right, 0)
    forward_w_out(left, 1)

    for chip in range(chips):
        _drain(sinner.at[chip, peers], inner_send.at[chip])

    def gate_rows(bp, carry):
        _drain(back.at[bp, peers], back_recv.at[bp])
        g = gate[bp].astype(F32)
        v = back[bp].astype(F32) * (g * jax.nn.sigmoid(g))
        for part in range(2):
            mine = v[:, part * 8 : (part + 1) * 8, :].reshape(nslot // 2, chans).astype(BF16)
            at = pl.ds(part * (E // 2), E // 2)
            sinner[bp, at] = mine.reshape(E // 2, 16, chans)
            target = 2 * bp + part

            @pl.when(target != c)
            def _():
                _remote(
                    sinner.at[bp, at],
                    gathered.at[c],
                    gated_send.at[target],
                    gated_recv.at[c],
                    context=target,
                ).start()

            @pl.when(target == c)
            def _():
                gathered[c] = mine.reshape(E // 2, 16, chans)

        return carry

    lax.fori_loop(0, chips, gate_rows, 0)
    forward_w_out(across, 2)

    for k in range(1, C):
        block = lax.rem(c + k, C)
        _drain(gathered.at[block], gated_recv.at[block])
    for k in range(chips):
        block = lax.rem(x + k, chips) * 2 + 1 - core
        _drain(w_out.at[block], wout_recv.at[2, block])
    parts, _, _, fin_n = fin_src.shape

    def finish(j, carry):
        total = jnp.zeros((nrow, 2 * fin_n), F32)
        cols = pl.ds(pl.multiple_of(j * 2 * fin_n, 2 * fin_n), 2 * fin_n)
        for block in range(C):
            total = total + _dot(gathered[block].reshape(nrow, chans), w_out[block, :, cols])
        fin_src[j] = _fold(total[:, :fin_n], total[:, fin_n:])
        _scatter_expert(E, fin_src.at[j], fin_dst.at[j], fin_send.at[j], fin_recv.at[j])
        return carry

    lax.fori_loop(0, parts, finish, 0)

    places = [_slot_onehot(row, nslot, part) for part in range(2)]
    for j in range(parts):
        _drain(fin_dst.at[j, peers], fin_recv.at[j])
        arrived = fin_dst[j].reshape(nslot, fin_n)
        for part in range(2):
            begin = (2 * j + part) * fin_n
            out[:, begin : begin + fin_n] = _dot(places[part], arrived, ((0,), (0,))).astype(BF16)

    for h in range(2):
        _drain(stok.at[h, peers], tok_send.at[h])
        for k in range(3):
            _drain(rows.at[h, 0], row_send.at[h, k])
            _drain(rows.at[h, 0], fwd_send.at[h, k])
        _drain(rows.at[h, 0], hop_send.at[h])
    _drain(wstep_all.at[pl.ds(0, C - 1)], step_send)
    _drain(sss.at[peers], ss_send)
    _drain(ss.at[pl.ds(0, C - 1)], pos_send)
    for chip in range(chips):
        _drain(sback.at[chip, peers], back_send.at[chip])
    for k in range(1, C):
        target = lax.rem(c + k, C)
        _drain(gathered.at[0], gated_send.at[target])
    for j in range(parts):
        _drain(fin_src.at[j, peers], fin_send.at[j])
    for k in range(1, chips):
        _drain(w_out.at[0, pl.ds(0, early)], wout_send.at[0, k])
        _drain(w_out.at[0, pl.ds(early, w_out.shape[1] - early)], wout_send.at[1, k])
    _drain(w_out.at[0], wout_send.at[0, 0])
    _drain(w_out.at[0], wout_send.at[1, 0])
    _drain(w_out.at[0], fwd_send.at[0, 3])
    _drain(w_out.at[0], fwd_send.at[1, 3])


def per_device(
    tokens,
    route,
    w_inner,
    w_state,
    w_step,
    step_bias,
    decay_log,
    skip_gain,
    conv_weight,
    conv_bias,
    w_out,
):
    T, width = tokens.shape[1:]
    E, C = lax.axis_size("expert"), lax.axis_size("context")
    chips = C // 2
    chans = w_inner.shape[3]
    wide = w_state.shape[2] + C * 16
    parts = 4
    fin_n = width // parts // 2
    vmem = pl.BlockSpec(memory_space=pltpu.VMEM)
    hbm = pl.BlockSpec(memory_space=pl.ANY)
    dma = pltpu.SemaphoreType.DMA
    flat = pltpu.VMEM((chips, E, 16, chans), BF16)
    mixed = pl.pallas_call(
        functools.partial(layer_kernel, E, C),
        out_shape=jax.ShapeDtypeStruct((T, width), BF16),
        in_specs=[vmem, vmem, hbm, vmem, vmem, vmem, vmem, vmem, vmem, vmem, hbm],
        out_specs=vmem,
        scratch_shapes=[
            pltpu.VMEM((C, T), jnp.int32),
            pltpu.VMEM((2, width // 4, 2, chans), BF16),
            pltpu.VMEM((2, width, chans), BF16),
            pltpu.VMEM((C, chans, width), BF16),
            pltpu.VMEM((2, E, 16, width // 4), BF16),
            pltpu.VMEM((2, E, 16, width // 4), BF16),
            pltpu.VMEM((2, C, E * 8, width // 2), BF16),
            flat,
            flat,
            flat,
            flat,
            flat,
            pltpu.VMEM((C, 16, width), BF16),
            pltpu.VMEM((E, 16, wide), BF16),
            pltpu.VMEM((E, 16, wide), BF16),
            pltpu.VMEM((C, T, wide), BF16),
            pltpu.VMEM((C, E // 2, 16, chans), BF16),
            pltpu.VMEM((parts, E, 16, fin_n), BF16),
            pltpu.VMEM((parts, E, 16, fin_n), BF16),
            pltpu.VMEM((HEAD_DIM, chans), F32),
            pltpu.VMEM((8, chans), F32),
            pltpu.VMEM((2, T, chans), BF16),
            dma((2,)),
            dma,
            dma((2,)),
            dma((2,)),
            dma,
            dma,
            dma((2, 3)),
            dma((2, C)),
            dma((2, 4)),
            dma((2,)),
            dma,
            dma,
            dma,
            dma,
            dma((chips,)),
            dma((chips,)),
            dma((2, chips)),
            dma((3, C)),
            dma((chips,)),
            dma((chips,)),
            dma((C,)),
            dma((C,)),
            dma((parts,)),
            dma((parts,)),
        ],
        compiler_params=pltpu.CompilerParams(
            collective_id=0, has_side_effects=True, vmem_limit_bytes=VMEM_LIMIT
        ),
        name="layer",
    )(
        route[0, :, 0].reshape(C, T),
        tokens[0],
        w_inner[0],
        w_state[0],
        w_step[0].T,
        step_bias[None, :],
        decay_log[None, :],
        skip_gain[None, :],
        conv_weight,
        conv_bias[None, :],
        w_out[0],
    )
    return mixed[None]


def solution(mesh):
    in_specs = (
        P("expert", "context", None),
        P("expert", None, None),
        P("expert", None, None, "context"),
        P("expert", None, None),
        P("expert", None, "context"),
        P("context"),
        P("context"),
        P("context"),
        P(None, "context"),
        P("context"),
        P("expert", "context", None),
    )
    out_specs = P("expert", "context", None)
    return jax.shard_map(
        per_device, mesh=mesh, in_specs=in_specs, out_specs=out_specs, check_vma=False
    )
```

```python
import functools

import jax
import jax.numpy as jnp
from jax import lax
from jax.experimental import pallas as pl
from jax.experimental.pallas import tpu as pltpu
from jax.sharding import PartitionSpec as P

HEAD_DIM = 64
MESH = pl.DeviceIdType.MESH
F32 = jnp.float32
BF16 = jnp.bfloat16
VMEM_LIMIT = 60 * 1024 * 1024


def _dot(a, b, dims=((1,), (0,)), precision=None):
    return lax.dot_general(a, b, (dims, ((), ())), precision=precision, preferred_element_type=F32)


def _greet(expert_peers, context_peers):
    e, c = lax.axis_index("expert"), lax.axis_index("context")
    barrier = pltpu.get_barrier_semaphore()

    def greet(axis, me, count):
        def body(k, carry):
            peer = lax.rem(me + k, count)
            pl.semaphore_signal(barrier, inc=1, device_id={axis: peer}, device_id_type=MESH)
            return carry

        lax.fori_loop(1, count, body, 0)

    greet("expert", e, expert_peers)
    greet("context", c, context_peers)


def _meet(expert_peers, context_peers):
    pl.semaphore_wait(pltpu.get_barrier_semaphore(), expert_peers + context_peers - 2)


def _drain(ref, sem):
    pltpu.make_async_copy(ref, ref, sem).wait()


def _fold(top, bottom):
    n, w = top.shape[0] // 8, top.shape[1]
    return jnp.concatenate([top.reshape(n, 8, w), bottom.reshape(n, 8, w)], axis=1).astype(BF16)


def _unfold(folded):
    n, _, w = folded.shape
    wide = folded.astype(F32)
    return (
        wide[:, :8, :].reshape(n * 8, w).astype(BF16),
        wide[:, 8:, :].reshape(n * 8, w).astype(BF16),
    )


def _scatter_expert(E, src, dst, send_sem, recv_sem):
    e = lax.axis_index("expert")

    def body(k, carry):
        peer = lax.rem(e + k, E)
        pltpu.make_async_remote_copy(
            src_ref=src.at[peer],
            dst_ref=dst.at[e],
            send_sem=send_sem,
            recv_sem=recv_sem,
            device_id={"expert": peer},
            device_id_type=MESH,
        ).start()
        return carry

    lax.fori_loop(1, E, body, 0)
    dst[e] = src[e]


def _slot_onehot(row, n, half):
    place = row + (row & -8) + 8 * half
    return (lax.broadcasted_iota(jnp.int32, (n, row.shape[1]), 0) == place).astype(BF16)


def _remote(src, dst, send_sem, recv_sem, **where):
    return pltpu.make_async_remote_copy(
        src_ref=src,
        dst_ref=dst,
        send_sem=send_sem,
        recv_sem=recv_sem,
        device_id=where,
        device_id_type=MESH,
    )


def _softplus(v):
    return jnp.maximum(v, 0.0) + jnp.log1p(jnp.exp(-jnp.abs(v)))


def _iota(shape, axis):
    return lax.broadcasted_iota(jnp.int32, shape, axis)


def layer_kernel(
    E,
    C,
    ids,
    tokens,
    w_inner_hbm,
    w_state,
    w_step,
    step_bias,
    decay_log,
    skip_gain,
    conv_weight,
    conv_bias,
    w_out_hbm,
    out,
    slots,
    w3,
    w_inner,
    w_out,
    stok,
    rtok,
    rows,
    sinner,
    inner,
    gate,
    sback,
    back,
    wstep_all,
    sss,
    rss,
    ss,
    gathered,
    fin_src,
    fin_dst,
    state,
    tail8,
    scanned,
    w3_sem,
    w_sem,
    tok_send,
    tok_recv,
    step_send,
    step_recv,
    row_send,
    row_recv,
    fwd_send,
    hop_send,
    ss_send,
    ss_recv,
    pos_send,
    pos_recv,
    inner_send,
    inner_recv,
    wout_send,
    wout_recv,
    back_send,
    back_recv,
    gated_send,
    gated_recv,
    fin_send,
    fin_recv,
):
    e, c = lax.axis_index("expert"), lax.axis_index("context")
    x, core = c // 2, lax.rem(c, 2)
    sibling = c + 1 - 2 * core
    chips = C // 2
    T, width = tokens.shape
    half = width // 2
    quarter = width // 4
    chans = inner.shape[3]
    nrow = E * 8
    nslot = E * 16
    heads = w_step.shape[0]
    pieces, piece = w3.shape[0], w3.shape[1]
    count = width // piece
    depth = w_out.shape[1]
    early = depth // 16 * 5
    peers = pl.ds(0, E - 1)

    def load_piece(q):
        return pltpu.make_async_copy(
            w_inner_hbm.at[pl.ds(q * piece, piece)], w3.at[q % pieces], w3_sem.at[q % pieces]
        )

    _greet(E, C)
    for q in range(pieces):
        load_piece(q).start()
    load_w_out = pltpu.make_async_copy(w_out_hbm, w_out.at[c], w_sem)
    load_w_out.start()

    values = ids[...].astype(F32)
    eye = (_iota((T, T), 0) == _iota((T, T), 1)).astype(BF16)
    columns = _dot(eye, values.astype(BF16), ((1,), (1,)))
    earlier = _iota((T, T), 0) < _iota((T, T), 1)
    for b in range(C):
        same = (columns[:, b : b + 1] == values[b : b + 1, :]) & earlier
        rank = jnp.sum(same.astype(F32), axis=0, keepdims=True)
        slots[b : b + 1, :] = ids[b : b + 1, :] * 8 + rank.astype(jnp.int32)

    row = slots[pl.ds(c, 1), :]
    dispatch = (_iota((nrow, T), 0) == row).astype(BF16)

    def pack(h):
        a = h * half
        stok[h] = _fold(
            _dot(dispatch, tokens[:, a : a + quarter]),
            _dot(dispatch, tokens[:, a + quarter : a + half]),
        )

    pack(0)
    _meet(E, C)
    _scatter_expert(E, stok.at[0], rtok.at[0], tok_send.at[0], tok_recv.at[0])
    pack(1)
    _scatter_expert(E, stok.at[1], rtok.at[1], tok_send.at[1], tok_recv.at[1])

    def share(ref, send_sem, recv_sem):
        def body(k, carry):
            peer = lax.rem(c + k, C)
            _remote(ref.at[c], ref.at[c], send_sem, recv_sem, context=peer).start()
            return carry

        lax.fori_loop(1, C, body, 0)

    wide = w_step[...].astype(F32)
    wstep_all[c] = jnp.concatenate([wide, jnp.zeros((16 - heads, width), F32)], axis=0).astype(BF16)
    share(wstep_all, step_send, step_recv)

    right = lax.rem(x + 1, chips) * 2 + core
    left = lax.rem(x + chips - 1, chips) * 2 + core
    across = lax.rem(x + chips // 2, chips) * 2 + core

    def send_w_out(block, where, target, sem, kind):
        return _remote(
            w_out.at[block, where], w_out.at[block, where], sem, wout_recv.at[kind, block], context=target
        )

    def await_w_out(block, where, kind):
        _drain(w_out.at[block, where], wout_recv.at[kind, block])

    first_part, last_part, all_parts = pl.ds(0, early), pl.ds(early, depth - early), pl.ds(0, depth)
    load_w_out.wait()
    send_w_out(c, first_part, right, wout_send.at[0], 0).start()
    send_w_out(c, first_part, left, wout_send.at[1], 0).start()

    for q in range(count):
        load_piece(q).wait()

        def part_w(i, carry):
            block = w3[q % pieces, pl.ds(i * 128, 128)]
            at = pl.ds(pl.multiple_of(q * piece + i * 128, 128), 128)
            w_inner[0, at, :] = block[:, 0, :]
            w_inner[1, at, :] = block[:, 1, :]
            return carry

        lax.fori_loop(0, piece // 128, part_w, 0)
        if q + pieces < count:
            load_piece(q + pieces).start()

    def send_rows(h, block, target, sem):
        return _remote(rows.at[h, block], rows.at[h, block], sem, row_recv.at[h, block], context=target)

    def await_rows(h, block):
        _drain(rows.at[h, block], row_recv.at[h, block])

    for h in range(2):
        _drain(rtok.at[h, peers], tok_recv.at[h])
        first_q, second_q = _unfold(rtok[h])
        rows[h, c, :, :quarter] = first_q
        rows[h, c, :, quarter:] = second_q
        send_rows(h, c, right, row_send.at[h, 0]).start()
        send_rows(h, c, left, row_send.at[h, 1]).start()
        send_rows(h, c, sibling, row_send.at[h, 2]).start()

    step_n = min(256, chans)

    def project(chip, which, dst):
        first = rows[0, pl.ds(chip * 2, 2)].reshape(2 * nrow, half)
        second = rows[1, pl.ds(chip * 2, 2)].reshape(2 * nrow, half)
        for n in range(chans // step_n):
            cols = slice(n * step_n, (n + 1) * step_n)
            res = _dot(first, w_inner[which, :half, cols]) + _dot(second, w_inner[which, half:, cols])
            dst[chip, :, :, cols] = _fold(res[:nrow], res[nrow:])

    def inner_chip(chip):
        for h in range(2):
            await_rows(h, chip * 2 + 1 - core)
        project(chip, 1, sinner)
        _scatter_expert(E, sinner.at[chip], inner.at[chip], inner_send.at[chip], inner_recv.at[chip])

    await_rows(0, left)
    send_rows(0, left, right, hop_send.at[0]).start()
    send_rows(0, left, sibling, fwd_send.at[0, 0]).start()
    await_rows(0, right)
    send_rows(0, right, sibling, fwd_send.at[0, 1]).start()
    inner_chip(x)
    await_rows(1, right)
    send_rows(1, right, left, hop_send.at[1]).start()
    send_rows(1, right, sibling, fwd_send.at[1, 1]).start()
    await_rows(1, left)
    send_rows(1, left, sibling, fwd_send.at[1, 0]).start()

    _drain(wstep_all.at[pl.ds(0, C - 1)], step_recv)
    states, steps = [], []
    for h in range(2):
        mine = rows[h, c]
        at = slice(h * half, (h + 1) * half)
        step_w = wstep_all[:, :, at].reshape(C * 16, half)
        states.append(_dot(mine, w_state[at, :]))
        steps.append(_dot(mine, step_w, ((1,), (1,))))
    sss[...] = _fold(states[0] + states[1], steps[0] + steps[1])
    _scatter_expert(E, sss, rss, ss_send, ss_recv)

    second = 1 - lax.rem(x, 2)
    third = jnp.where(x < 2, 2, x - 2)

    def other_chip(i, carry):
        chip = jnp.where(i == 0, second, jnp.where(i == 1, third, 6 - x - second - third))

        @pl.when(i == 1)
        def _():
            for h in range(2):
                await_rows(h, across)
                send_rows(h, across, sibling, fwd_send.at[h, 2]).start()
            _drain(rss.at[peers], ss_recv)
            vectors = rss[...].reshape(nslot, rss.shape[2])
            at_state = _dot(_slot_onehot(row, nslot, 0), vectors, ((0,), (0,)))
            at_step = _dot(_slot_onehot(row, nslot, 1), vectors, ((0,), (0,)))
            ss[c] = jnp.concatenate([at_state, at_step], axis=1).astype(BF16)
            share(ss, pos_send, pos_recv)

        inner_chip(chip)
        return carry

    lax.fori_loop(0, chips - 1, other_chip, 0)

    send_w_out(c, last_part, right, wout_send.at[2], 1).start()
    send_w_out(c, last_part, left, wout_send.at[3], 1).start()
    send_w_out(c, all_parts, sibling, wout_send.at[4], 2).start()

    def gate_chip(chip, carry):
        project(chip, 0, gate)
        return carry

    lax.fori_loop(0, chips, gate_chip, 0)

    exact = lax.Precision.HIGHEST
    taps = conv_weight.shape[0]
    nbc = HEAD_DIM
    state[...] = jnp.zeros_like(state)
    tail8[...] = jnp.zeros_like(tail8)
    lower = _iota((T, T), 0) >= _iota((T, T), 1)
    lower_one = lower.astype(F32)
    upper_one = (_iota((T, T), 0) <= _iota((T, T), 1)).astype(F32)
    first = _iota((T, 2 * HEAD_DIM), 1) < HEAD_DIM
    lanes = C * 16
    pick = (_iota((lanes, heads), 0) == c * 16 + _iota((lanes, heads), 1)).astype(BF16)
    pick_t = (_iota((heads, lanes), 1) == c * 16 + _iota((heads, lanes), 0)).astype(BF16)
    diagonal = _iota((heads, heads), 0) == _iota((heads, heads), 1)

    def column(v):
        return jnp.sum(jnp.where(diagonal, v, 0.0), axis=1, keepdims=True)

    bias_l, rate_l = step_bias[...], -jnp.exp(decay_log[...])
    bias_r, rate_r = column(bias_l), column(rate_l)
    gain = skip_gain[...]

    def chunk(b, part):
        place = _slot_onehot(slots[pl.ds(b, 1), :], nslot, part)
        raw = _dot(place, inner[b // 2].reshape(nslot, chans), ((0,), (0,)))
        joined = jnp.concatenate([tail8[...], raw], axis=0)
        tail8[...] = raw[T - 8 :, :]
        conv = conv_bias[...] + jnp.zeros_like(raw)
        for j in range(taps):
            begin = 8 - taps + 1 + j
            conv = conv + conv_weight[j : j + 1, :] * joined[begin : begin + T, :]
        signal = conv * jax.nn.sigmoid(conv)

        mine = ss[b]
        keys, queries = mine[:, :nbc], mine[:, nbc : 2 * nbc]
        raw_step = mine[:, 2 * nbc :]
        steps = _softplus(_dot(raw_step, pick) + bias_l)
        steps_t = _softplus(_dot(pick_t, raw_step, ((1,), (1,))) + bias_r)
        summed = _dot(lower_one, steps * rate_l, precision=exact)
        summed_t = _dot(steps_t * rate_r, upper_one, precision=exact)
        scores = _dot(queries, keys, ((1,), (1,)))
        grown = jnp.exp(summed)
        end = summed[T - 1 : T, :]
        tail = jnp.exp(end - summed) * steps
        whole = jnp.exp(end)
        for pair in range(heads // 2):
            cols = slice(pair * 2 * HEAD_DIM, (pair + 1) * 2 * HEAD_DIM)
            xs = signal[:, cols]
            xb = xs.astype(BF16)
            weights = []
            for h in (2 * pair, 2 * pair + 1):
                gaps = summed[:, h : h + 1] - summed_t[h : h + 1, :]
                decay = jnp.exp(jnp.where(lower, gaps, -jnp.inf))
                weights.append((scores * decay * steps_t[h : h + 1, :]).astype(BF16))
            zero = jnp.zeros_like(xb)
            stacked = jnp.concatenate([jnp.where(first, xb, zero), jnp.where(first, zero, xb)], axis=0)
            local = _dot(jnp.concatenate(weights, axis=1), stacked)

            def spread(v):
                n = v.shape[0]
                a = jnp.broadcast_to(v[:, 2 * pair : 2 * pair + 1], (n, 2 * HEAD_DIM))
                z = jnp.broadcast_to(v[:, 2 * pair + 1 : 2 * pair + 2], (n, 2 * HEAD_DIM))
                return jnp.where(first[:n], a, z)

            old = state[:, cols]
            carried = spread(grown) * _dot(queries, old.astype(BF16))
            fed = (spread(tail) * xs).astype(BF16)
            state[:, cols] = spread(whole) * old + _dot(keys, fed, ((0,), (0,)))
            scanned[part, :, cols] = (local + carried + spread(gain) * xs).astype(BF16)

    _drain(ss.at[pl.ds(0, C - 1)], pos_recv)

    def pair_of_chunks(bp, carry):
        _drain(inner.at[bp, peers], inner_recv.at[bp])
        chunk(2 * bp, 0)
        chunk(2 * bp + 1, 1)
        total = None
        for part in range(2):
            place = _slot_onehot(slots[pl.ds(2 * bp + part, 1), :], nslot, part)
            term = _dot(place, scanned[part])
            total = term if total is None else total + term
        sback[bp] = total.astype(BF16).reshape(E, 16, chans)
        _scatter_expert(E, sback.at[bp], back.at[bp], back_send.at[bp], back_recv.at[bp])

        return carry

    lax.fori_loop(0, chips, pair_of_chunks, 0)

    hops = (pl.ds(0, depth // 2), pl.ds(depth // 2, depth // 2))
    for block in (left, right):
        await_w_out(block, first_part, 0)
        await_w_out(block, last_part, 1)
    send_w_out(left, hops[0], right, wout_send.at[5], 3).start()
    send_w_out(right, hops[1], left, wout_send.at[6], 4).start()
    send_w_out(left, all_parts, sibling, wout_send.at[7], 2).start()
    send_w_out(right, all_parts, sibling, wout_send.at[8], 2).start()

    for chip in range(chips):
        _drain(sinner.at[chip, peers], inner_send.at[chip])

    def gate_rows(bp, carry):
        _drain(back.at[bp, peers], back_recv.at[bp])
        g = gate[bp].astype(F32)
        v = back[bp].astype(F32) * (g * jax.nn.sigmoid(g))
        share_n = E // 4
        for part in range(2):
            mine = v[:, part * 8 : (part + 1) * 8, :].reshape(nslot // 2, chans).astype(BF16)
            sinner[bp, pl.ds(part * (E // 2), E // 2)] = mine.reshape(E // 2, 16, chans)

            @pl.when(2 * bp + part == c)
            def _():
                gathered[c] = sinner[bp, pl.ds(part * (E // 2), E // 2)]

        for group in range(2):
            for part in range(2):
                target = 2 * bp + part

                @pl.when(target != c)
                def _():
                    _remote(
                        sinner.at[bp, pl.ds((part * 2 + group) * share_n, share_n)],
                        gathered.at[c, pl.ds(group * share_n, share_n)],
                        gated_send.at[group, target],
                        gated_recv.at[group, c],
                        context=target,
                    ).start()

        @pl.when(bp == chips - 2)
        def _():
            await_w_out(across, hops[0], 3)
            await_w_out(across, hops[1], 4)
            send_w_out(across, all_parts, sibling, wout_send.at[9], 2).start()

        return carry

    lax.fori_loop(0, chips, gate_rows, 0)

    for k in range(chips):
        await_w_out(lax.rem(x + k, chips) * 2 + 1 - core, all_parts, 2)
    parts, _, _, fin_n = fin_src.shape
    seqs, share_n = E // 2, E // 4

    def finish(group, carry):
        for k in range(1, C):
            block = lax.rem(c + k, C)
            _drain(gathered.at[block, pl.ds(0, share_n)], gated_recv.at[group, block])

        def columns_of(j, carry):
            total = jnp.zeros((nrow // 2, 2 * fin_n), F32)
            cols = pl.ds(pl.multiple_of(j * 2 * fin_n, 2 * fin_n), 2 * fin_n)
            for block in range(C):
                mine = gathered[block, pl.ds(group * share_n, share_n)].reshape(nrow // 2, chans)
                total = total + _dot(mine, w_out[block, :, cols])
            fin_src[j, pl.ds(group * seqs, seqs)] = _fold(total[:, :fin_n], total[:, fin_n:])

            def send(k, carry):
                peer = group * seqs + lax.rem(e + k, seqs)

                @pl.when(peer != e)
                def _():
                    _remote(
                        fin_src.at[j, peer], fin_dst.at[j, e], fin_send.at[j], fin_recv.at[j], expert=peer
                    ).start()

                @pl.when(peer == e)
                def _():
                    fin_dst[j, e] = fin_src[j, e]

                return carry

            lax.fori_loop(0, seqs, send, 0)
            return carry

        lax.fori_loop(0, parts, columns_of, 0)
        return carry

    lax.fori_loop(0, 2, finish, 0)

    places = [_slot_onehot(row, nslot, part) for part in range(2)]
    for j in range(parts):
        _drain(fin_dst.at[j, peers], fin_recv.at[j])
        arrived = fin_dst[j].reshape(nslot, fin_n)
        for part in range(2):
            begin = (2 * j + part) * fin_n
            out[:, begin : begin + fin_n] = _dot(places[part], arrived, ((0,), (0,))).astype(BF16)

    for h in range(2):
        _drain(stok.at[h, peers], tok_send.at[h])
        for k in range(3):
            _drain(rows.at[h, 0], row_send.at[h, k])
            _drain(rows.at[h, 0], fwd_send.at[h, k])
        _drain(rows.at[h, 0], hop_send.at[h])
    _drain(wstep_all.at[pl.ds(0, C - 1)], step_send)
    _drain(sss.at[peers], ss_send)
    _drain(ss.at[pl.ds(0, C - 1)], pos_send)
    for chip in range(chips):
        _drain(sback.at[chip, peers], back_send.at[chip])
    for k in range(1, C):
        target = lax.rem(c + k, C)
        for group in range(2):
            _drain(gathered.at[0, pl.ds(0, share_n)], gated_send.at[group, target])
    for j in range(parts):
        _drain(fin_src.at[j, peers], fin_send.at[j])
    for k, where in enumerate((first_part, first_part, last_part, last_part, all_parts) + hops + (all_parts,) * 3):
        _drain(w_out.at[0, where], wout_send.at[k])


def per_device(
    tokens,
    route,
    w_inner,
    w_state,
    w_step,
    step_bias,
    decay_log,
    skip_gain,
    conv_weight,
    conv_bias,
    w_out,
):
    T, width = tokens.shape[1:]
    E, C = lax.axis_size("expert"), lax.axis_size("context")
    chips = C // 2
    chans = w_inner.shape[3]
    wide = w_state.shape[2] + C * 16
    parts = 4
    fin_n = width // parts // 2
    vmem = pl.BlockSpec(memory_space=pltpu.VMEM)
    hbm = pl.BlockSpec(memory_space=pl.ANY)
    dma = pltpu.SemaphoreType.DMA
    flat = pltpu.VMEM((chips, E, 16, chans), BF16)
    mixed = pl.pallas_call(
        functools.partial(layer_kernel, E, C),
        out_shape=jax.ShapeDtypeStruct((T, width), BF16),
        in_specs=[vmem, vmem, hbm, vmem, vmem, vmem, vmem, vmem, vmem, vmem, hbm],
        out_specs=vmem,
        scratch_shapes=[
            pltpu.VMEM((C, T), jnp.int32),
            pltpu.VMEM((2, width // 4, 2, chans), BF16),
            pltpu.VMEM((2, width, chans), BF16),
            pltpu.VMEM((C, chans, width), BF16),
            pltpu.VMEM((2, E, 16, width // 4), BF16),
            pltpu.VMEM((2, E, 16, width // 4), BF16),
            pltpu.VMEM((2, C, E * 8, width // 2), BF16),
            flat,
            flat,
            flat,
            flat,
            flat,
            pltpu.VMEM((C, 16, width), BF16),
            pltpu.VMEM((E, 16, wide // 2), BF16),
            pltpu.VMEM((E, 16, wide // 2), BF16),
            pltpu.VMEM((C, T, wide), BF16),
            pltpu.VMEM((C, E // 2, 16, chans), BF16),
            pltpu.VMEM((parts, E, 16, fin_n), BF16),
            pltpu.VMEM((parts, E, 16, fin_n), BF16),
            pltpu.VMEM((HEAD_DIM, chans), F32),
            pltpu.VMEM((8, chans), F32),
            pltpu.VMEM((2, T, chans), BF16),
            dma((2,)),
            dma,
            dma((2,)),
            dma((2,)),
            dma,
            dma,
            dma((2, 3)),
            dma((2, C)),
            dma((2, 3)),
            dma((2,)),
            dma,
            dma,
            dma,
            dma,
            dma((chips,)),
            dma((chips,)),
            dma((10,)),
            dma((5, C)),
            dma((chips,)),
            dma((chips,)),
            dma((2, C)),
            dma((2, C)),
            dma((parts,)),
            dma((parts,)),
        ],
        compiler_params=pltpu.CompilerParams(
            collective_id=0, has_side_effects=True, vmem_limit_bytes=VMEM_LIMIT
        ),
        name="layer",
    )(
        route[0, :, 0].reshape(C, T),
        tokens[0],
        w_inner[0],
        w_state[0],
        w_step[0].T,
        step_bias[None, :],
        decay_log[None, :],
        skip_gain[None, :],
        conv_weight,
        conv_bias[None, :],
        w_out[0],
    )
    return mixed[None]


def solution(mesh):
    in_specs = (
        P("expert", "context", None),
        P("expert", None, None),
        P("expert", None, None, "context"),
        P("expert", None, None),
        P("expert", None, "context"),
        P("context"),
        P("context"),
        P("context"),
        P(None, "context"),
        P("context"),
        P("expert", "context", None),
    )
    out_specs = P("expert", "context", None)
    return jax.shard_map(
        per_device, mesh=mesh, in_specs=in_specs, out_specs=out_specs, check_vma=False
    )
```

```python
import functools

import jax
import jax.numpy as jnp
from jax import lax
from jax.experimental import pallas as pl
from jax.experimental.pallas import tpu as pltpu
from jax.sharding import PartitionSpec as P

HEAD_DIM = 64
MESH = pl.DeviceIdType.MESH
F32 = jnp.float32
BF16 = jnp.bfloat16
VMEM_LIMIT = 60 * 1024 * 1024


def _dot(a, b, dims=((1,), (0,)), precision=None):
    return lax.dot_general(a, b, (dims, ((), ())), precision=precision, preferred_element_type=F32)


def _greet(expert_peers, context_peers):
    e, c = lax.axis_index("expert"), lax.axis_index("context")
    barrier = pltpu.get_barrier_semaphore()

    def greet(axis, me, count):
        def body(k, carry):
            peer = lax.rem(me + k, count)
            pl.semaphore_signal(barrier, inc=1, device_id={axis: peer}, device_id_type=MESH)
            return carry

        lax.fori_loop(1, count, body, 0)

    greet("expert", e, expert_peers)
    greet("context", c, context_peers)
    owner = e // (expert_peers // context_peers)

    def greet_owner(k, carry):
        @pl.when((k != e) | (owner != c))
        def _():
            pl.semaphore_signal(
                barrier, inc=1, device_id={"expert": k, "context": owner}, device_id_type=MESH
            )

        return carry

    lax.fori_loop(0, expert_peers, greet_owner, 0)


def _meet(expert_peers, context_peers):
    e, c = lax.axis_index("expert"), lax.axis_index("context")
    own = jnp.where(e // (expert_peers // context_peers) == c, 1, 0)
    pl.semaphore_wait(pltpu.get_barrier_semaphore(), 2 * expert_peers + context_peers - 2 - own)


def _drain(ref, sem):
    pltpu.make_async_copy(ref, ref, sem).wait()


def _fold(top, bottom):
    n, w = top.shape[0] // 8, top.shape[1]
    return jnp.concatenate([top.reshape(n, 8, w), bottom.reshape(n, 8, w)], axis=1).astype(BF16)


def _unfold(folded):
    n, _, w = folded.shape
    wide = folded.astype(F32)
    return (
        wide[:, :8, :].reshape(n * 8, w).astype(BF16),
        wide[:, 8:, :].reshape(n * 8, w).astype(BF16),
    )


def _scatter_expert(E, src, dst, send_sem, recv_sem):
    e = lax.axis_index("expert")

    def body(k, carry):
        peer = lax.rem(e + k, E)
        pltpu.make_async_remote_copy(
            src_ref=src.at[peer],
            dst_ref=dst.at[e],
            send_sem=send_sem,
            recv_sem=recv_sem,
            device_id={"expert": peer},
            device_id_type=MESH,
        ).start()
        return carry

    lax.fori_loop(1, E, body, 0)
    dst[e] = src[e]


def _slot_onehot(row, n, half):
    place = row + (row & -8) + 8 * half
    return (lax.broadcasted_iota(jnp.int32, (n, row.shape[1]), 0) == place).astype(BF16)


def _remote(src, dst, send_sem, recv_sem, **where):
    return pltpu.make_async_remote_copy(
        src_ref=src,
        dst_ref=dst,
        send_sem=send_sem,
        recv_sem=recv_sem,
        device_id=where,
        device_id_type=MESH,
    )


def _softplus(v):
    return jnp.maximum(v, 0.0) + jnp.log1p(jnp.exp(-jnp.abs(v)))


def _iota(shape, axis):
    return lax.broadcasted_iota(jnp.int32, shape, axis)


def layer_kernel(
    E,
    C,
    ids,
    tokens,
    w_inner_hbm,
    w_state,
    w_step,
    step_bias,
    decay_log,
    skip_gain,
    conv_weight,
    conv_bias,
    w_out_hbm,
    out,
    slots,
    w3,
    w_inner,
    w_out,
    stok,
    rtok,
    rows,
    sinner,
    inner,
    gate,
    sback,
    back,
    wstep_all,
    sss,
    rss,
    ss,
    gathered,
    fin_src,
    fin_dst,
    state,
    tail8,
    scanned,
    w3_sem,
    w_sem,
    tok_send,
    tok_recv,
    step_send,
    step_recv,
    row_send,
    row_recv,
    fwd_send,
    hop_send,
    ss_send,
    ss_recv,
    pos_send,
    pos_recv,
    inner_send,
    inner_recv,
    wout_send,
    wout_recv,
    across_send,
    back_send,
    back_recv,
    gated_send,
    gated_recv,
    fin_send,
    fin_recv,
):
    e, c = lax.axis_index("expert"), lax.axis_index("context")
    x, core = c // 2, lax.rem(c, 2)
    sibling = c + 1 - 2 * core
    chips = C // 2
    T, width = tokens.shape
    half = width // 2
    quarter = width // 4
    chans = inner.shape[3]
    nrow = E * 8
    nslot = E * 16
    heads = w_step.shape[0]
    pieces, piece = w3.shape[0], w3.shape[1]
    count = width // piece
    depth = w_out.shape[1]
    early = depth // 16 * 4
    peers = pl.ds(0, E - 1)

    def load_piece(q):
        return pltpu.make_async_copy(
            w_inner_hbm.at[pl.ds(q * piece, piece)], w3.at[q % pieces], w3_sem.at[q % pieces]
        )

    _greet(E, C)
    for q in range(pieces):
        load_piece(q).start()
    load_w_out = pltpu.make_async_copy(w_out_hbm, w_out.at[c], w_sem)
    load_w_out.start()

    values = ids[...].astype(F32)
    eye = (_iota((T, T), 0) == _iota((T, T), 1)).astype(BF16)
    columns = _dot(eye, values.astype(BF16), ((1,), (1,)))
    earlier = _iota((T, T), 0) < _iota((T, T), 1)
    for b in range(C):
        same = (columns[:, b : b + 1] == values[b : b + 1, :]) & earlier
        rank = jnp.sum(same.astype(F32), axis=0, keepdims=True)
        slots[b : b + 1, :] = ids[b : b + 1, :] * 8 + rank.astype(jnp.int32)

    row = slots[pl.ds(c, 1), :]
    dispatch = (_iota((nrow, T), 0) == row).astype(BF16)

    def pack(h):
        a = h * half
        stok[h] = _fold(
            _dot(dispatch, tokens[:, a : a + quarter]),
            _dot(dispatch, tokens[:, a + quarter : a + half]),
        )

    pack(0)
    _meet(E, C)
    _scatter_expert(E, stok.at[0], rtok.at[0], tok_send.at[0], tok_recv.at[0])
    pack(1)
    _scatter_expert(E, stok.at[1], rtok.at[1], tok_send.at[1], tok_recv.at[1])

    def share(ref, send_sem, recv_sem):
        def body(k, carry):
            peer = lax.rem(c + k, C)
            _remote(ref.at[c], ref.at[c], send_sem, recv_sem, context=peer).start()
            return carry

        lax.fori_loop(1, C, body, 0)

    wide = w_step[...].astype(F32)
    wstep_all[c] = jnp.concatenate([wide, jnp.zeros((16 - heads, width), F32)], axis=0).astype(BF16)
    share(wstep_all, step_send, step_recv)

    right = lax.rem(x + 1, chips) * 2 + core
    left = lax.rem(x + chips - 1, chips) * 2 + core
    across = lax.rem(x + chips // 2, chips) * 2 + core

    def send_w_out(block, where, target, sem, kind):
        return _remote(
            w_out.at[block, where], w_out.at[block, where], sem, wout_recv.at[kind, block], context=target
        )

    def await_w_out(block, where, kind):
        _drain(w_out.at[block, where], wout_recv.at[kind, block])

    first_part, next_part = pl.ds(0, early), pl.ds(early, depth // 2 - early)
    last_part, all_parts = pl.ds(depth // 2, depth // 2), pl.ds(0, depth)
    hops = (pl.ds(0, depth // 2), last_part)
    load_w_out.wait()
    send_w_out(c, first_part, right, wout_send.at[0], 0).start()
    send_w_out(c, first_part, left, wout_send.at[1], 0).start()

    for q in range(count):
        load_piece(q).wait()

        def part_w(i, carry):
            block = w3[q % pieces, pl.ds(i * 128, 128)]
            at = pl.ds(pl.multiple_of(q * piece + i * 128, 128), 128)
            w_inner[0, at, :] = block[:, 0, :]
            w_inner[1, at, :] = block[:, 1, :]
            return carry

        lax.fori_loop(0, piece // 128, part_w, 0)
        if q + pieces < count:
            load_piece(q + pieces).start()

    def send_rows(h, block, target, sem):
        return _remote(rows.at[h, block], rows.at[h, block], sem, row_recv.at[h, block], context=target)

    def await_rows(h, block):
        _drain(rows.at[h, block], row_recv.at[h, block])

    for h in range(2):
        _drain(rtok.at[h, peers], tok_recv.at[h])
        first_q, second_q = _unfold(rtok[h])
        rows[h, c, :, :quarter] = first_q
        rows[h, c, :, quarter:] = second_q
        send_rows(h, c, right, row_send.at[h, 0]).start()
        send_rows(h, c, left, row_send.at[h, 1]).start()
        send_rows(h, c, sibling, row_send.at[h, 2]).start()

    _drain(wstep_all.at[pl.ds(0, C - 1)], step_recv)
    states, steps = [], []
    for h in range(2):
        mine = rows[h, c]
        at = slice(h * half, (h + 1) * half)
        step_w = wstep_all[:, :, at].reshape(C * 16, half)
        states.append(_dot(mine, w_state[at, :]))
        steps.append(_dot(mine, step_w, ((1,), (1,))))
    sss[...] = _fold(states[0] + states[1], steps[0] + steps[1])
    _scatter_expert(E, sss, rss, ss_send, ss_recv)

    step_n = min(256, chans)

    def project(chip, which, dst):
        first = rows[0, pl.ds(chip * 2, 2)].reshape(2 * nrow, half)
        second = rows[1, pl.ds(chip * 2, 2)].reshape(2 * nrow, half)
        for n in range(chans // step_n):
            cols = slice(n * step_n, (n + 1) * step_n)
            res = _dot(first, w_inner[which, :half, cols]) + _dot(second, w_inner[which, half:, cols])
            dst[chip, :, :, cols] = _fold(res[:nrow], res[nrow:])

    def inner_chip(chip):
        for h in range(2):
            await_rows(h, chip * 2 + 1 - core)
        project(chip, 1, sinner)
        _scatter_expert(E, sinner.at[chip], inner.at[chip], inner_send.at[chip], inner_recv.at[chip])

    inner_chip(x)
    await_rows(0, left)
    send_rows(0, left, right, hop_send.at[0]).start()
    send_rows(0, left, sibling, fwd_send.at[0, 0]).start()
    await_rows(0, right)
    send_rows(0, right, sibling, fwd_send.at[0, 1]).start()
    await_rows(1, right)
    send_rows(1, right, left, hop_send.at[1]).start()
    send_rows(1, right, sibling, fwd_send.at[1, 1]).start()
    await_rows(1, left)
    send_rows(1, left, sibling, fwd_send.at[1, 0]).start()

    _drain(rss.at[peers], ss_recv)
    vectors = rss[...].reshape(nslot, rss.shape[2])
    at_state = _dot(_slot_onehot(row, nslot, 0), vectors, ((0,), (0,)))
    at_step = _dot(_slot_onehot(row, nslot, 1), vectors, ((0,), (0,)))
    ss[c] = jnp.concatenate([at_state, at_step], axis=1).astype(BF16)
    share(ss, pos_send, pos_recv)

    send_w_out(c, next_part, right, wout_send.at[9], 5).start()
    send_w_out(c, last_part, left, wout_send.at[3], 1).start()
    send_w_out(c, last_part, right, wout_send.at[2], 1).start()
    send_w_out(c, next_part, left, wout_send.at[10], 5).start()
    send_w_out(c, all_parts, sibling, wout_send.at[4], 2).start()

    second = 1 - lax.rem(x, 2)
    third = jnp.where(x < 2, 2, x - 2)

    def other_chip(i, carry):
        chip = jnp.where(i == 0, second, jnp.where(i == 1, third, 6 - x - second - third))

        @pl.when(i == 1)
        def _():
            for h in range(2):
                await_rows(h, across)
                send_rows(h, across, sibling, fwd_send.at[h, 2]).start()

        inner_chip(chip)
        return carry

    lax.fori_loop(0, chips - 1, other_chip, 0)

    def gate_chip(chip, carry):
        project(chip, 0, gate)
        return carry

    lax.fori_loop(0, chips, gate_chip, 0)

    exact = lax.Precision.HIGHEST
    taps = conv_weight.shape[0]
    nbc = HEAD_DIM
    state[...] = jnp.zeros_like(state)
    tail8[...] = jnp.zeros_like(tail8)
    lower = _iota((T, T), 0) >= _iota((T, T), 1)
    lower_one = lower.astype(F32)
    upper_one = (_iota((T, T), 0) <= _iota((T, T), 1)).astype(F32)
    first = _iota((T, 2 * HEAD_DIM), 1) < HEAD_DIM
    lanes = C * 16
    pick = (_iota((lanes, heads), 0) == c * 16 + _iota((lanes, heads), 1)).astype(BF16)
    pick_t = (_iota((heads, lanes), 1) == c * 16 + _iota((heads, lanes), 0)).astype(BF16)
    diagonal = _iota((heads, heads), 0) == _iota((heads, heads), 1)

    def column(v):
        return jnp.sum(jnp.where(diagonal, v, 0.0), axis=1, keepdims=True)

    bias_l, rate_l = step_bias[...], -jnp.exp(decay_log[...])
    bias_r, rate_r = column(bias_l), column(rate_l)
    gain = skip_gain[...]

    def chunk(b, part):
        place = _slot_onehot(slots[pl.ds(b, 1), :], nslot, part)
        raw = _dot(place, inner[b // 2].reshape(nslot, chans), ((0,), (0,)))
        joined = jnp.concatenate([tail8[...], raw], axis=0)
        tail8[...] = raw[T - 8 :, :]
        conv = conv_bias[...] + jnp.zeros_like(raw)
        for j in range(taps):
            begin = 8 - taps + 1 + j
            conv = conv + conv_weight[j : j + 1, :] * joined[begin : begin + T, :]
        signal = conv * jax.nn.sigmoid(conv)

        mine = ss[b]
        keys, queries = mine[:, :nbc], mine[:, nbc : 2 * nbc]
        raw_step = mine[:, 2 * nbc :]
        steps = _softplus(_dot(raw_step, pick) + bias_l)
        steps_t = _softplus(_dot(pick_t, raw_step, ((1,), (1,))) + bias_r)
        summed = _dot(lower_one, steps * rate_l, precision=exact)
        summed_t = _dot(steps_t * rate_r, upper_one, precision=exact)
        scores = _dot(queries, keys, ((1,), (1,)))
        grown = jnp.exp(summed)
        end = summed[T - 1 : T, :]
        tail = jnp.exp(end - summed) * steps
        whole = jnp.exp(end)
        for pair in range(heads // 2):
            cols = slice(pair * 2 * HEAD_DIM, (pair + 1) * 2 * HEAD_DIM)
            xs = signal[:, cols]
            xb = xs.astype(BF16)
            weights = []
            for h in (2 * pair, 2 * pair + 1):
                gaps = summed[:, h : h + 1] - summed_t[h : h + 1, :]
                decay = jnp.exp(jnp.where(lower, gaps, -jnp.inf))
                weights.append((scores * decay * steps_t[h : h + 1, :]).astype(BF16))
            zero = jnp.zeros_like(xb)
            stacked = jnp.concatenate([jnp.where(first, xb, zero), jnp.where(first, zero, xb)], axis=0)
            local = _dot(jnp.concatenate(weights, axis=1), stacked)

            def spread(v):
                n = v.shape[0]
                a = jnp.broadcast_to(v[:, 2 * pair : 2 * pair + 1], (n, 2 * HEAD_DIM))
                z = jnp.broadcast_to(v[:, 2 * pair + 1 : 2 * pair + 2], (n, 2 * HEAD_DIM))
                return jnp.where(first[:n], a, z)

            old = state[:, cols]
            carried = spread(grown) * _dot(queries, old.astype(BF16))
            fed = (spread(tail) * xs).astype(BF16)
            state[:, cols] = spread(whole) * old + _dot(keys, fed, ((0,), (0,)))
            scanned[part, :, cols] = (local + carried + spread(gain) * xs).astype(BF16)

    _drain(ss.at[pl.ds(0, C - 1)], pos_recv)

    def pair_of_chunks(bp, carry):
        _drain(inner.at[bp, peers], inner_recv.at[bp])

        @pl.when(bp == chips - 1)
        def _():
            await_w_out(left, first_part, 0)
            await_w_out(left, next_part, 5)
            send_w_out(left, hops[0], right, wout_send.at[5], 3).start()
            await_w_out(right, last_part, 1)
            send_w_out(right, hops[1], left, wout_send.at[6], 4).start()

        chunk(2 * bp, 0)
        chunk(2 * bp + 1, 1)
        total = None
        for part in range(2):
            place = _slot_onehot(slots[pl.ds(2 * bp + part, 1), :], nslot, part)
            term = _dot(place, scanned[part])
            total = term if total is None else total + term
        sback[bp] = total.astype(BF16).reshape(E, 16, chans)
        _scatter_expert(E, sback.at[bp], back.at[bp], back_send.at[bp], back_recv.at[bp])

        return carry

    lax.fori_loop(0, chips, pair_of_chunks, 0)

    for chip in range(chips):
        _drain(sinner.at[chip, peers], inner_send.at[chip])

    group = E // C

    def gate_rows(bp, carry):
        _drain(back.at[bp, peers], back_recv.at[bp])
        g = gate[bp].astype(F32)
        v = back[bp].astype(F32) * (g * jax.nn.sigmoid(g))
        sinner[bp] = v.astype(BF16)

        def send(k, carry):
            target = lax.rem(c + k, C)
            _remote(
                sinner.at[bp, pl.ds(target * group, group)],
                gathered.at[bp, c],
                gated_send.at[bp],
                gated_recv.at[bp],
                context=target,
            ).start()
            return carry

        lax.fori_loop(1, C, send, 0)
        gathered[bp, c] = sinner[bp, pl.ds(c * group, group)]
        return carry

    half_n = half // 2

    def multiply(bp, carry):
        _drain(gathered.at[bp, pl.ds(0, C - 1)], gated_recv.at[bp])

        def columns_of(j, carry):
            sums = []
            for late in range(2):
                total = jnp.zeros((group * 16, half_n), F32)
                cols = pl.ds(pl.multiple_of(late * half + j * half_n, half_n), half_n)
                for block in range(C):
                    mine = gathered[bp, block].reshape(group * 16, chans)
                    total = total + _dot(mine, w_out[block, :, cols])
                sums.append(total)
            fin_src[bp, :, :, pl.ds(pl.multiple_of(j * half_n, half_n), half_n)] = _fold(*sums)
            return carry

        lax.fori_loop(0, 2, columns_of, 0)
        return carry

    def send_final(bp, carry):
        def send(q, carry):
            seq, block = c * group + q // 2, 2 * bp + lax.rem(q, 2)
            here = (seq == e) & (block == c)

            @pl.when(jnp.logical_not(here))
            def _():
                _remote(
                    fin_src.at[bp, q],
                    fin_dst.at[e],
                    fin_send.at[bp * 2 * group + q],
                    fin_recv.at[e],
                    expert=seq,
                    context=block,
                ).start()

            @pl.when(here)
            def _():
                fin_dst[e] = fin_src[bp, q]

            return carry

        lax.fori_loop(0, 2 * group, send, 0)
        return carry

    await_w_out(right, first_part, 0)
    await_w_out(right, next_part, 5)
    send_w_out(right, all_parts, sibling, wout_send.at[8], 2).start()
    await_w_out(left, last_part, 1)
    send_w_out(left, all_parts, sibling, wout_send.at[7], 2).start()
    lax.fori_loop(0, chips - 1, gate_rows, 0)
    for k in range(2):
        await_w_out(across, hops[k], 3 + k)
        send_w_out(across, hops[k], sibling, across_send.at[k], 3 + k).start()
    gate_rows(chips - 1, 0)
    for block in (sibling, left + 1 - 2 * core, right + 1 - 2 * core):
        await_w_out(block, all_parts, 2)
    for k in range(2):
        await_w_out(across + 1 - 2 * core, hops[k], 3 + k)
    lax.fori_loop(0, chips - 2, multiply, 0)
    lax.fori_loop(0, chips - 2, send_final, 0)

    def last_blocks(bp, carry):
        multiply(bp, 0)
        send_final(bp, 0)
        return carry

    lax.fori_loop(chips - 2, chips, last_blocks, 0)

    places = [_slot_onehot(row, nslot, part) for part in range(2)]
    at_owner = c == e // group

    def await_final(k, carry):
        @pl.when(jnp.logical_not((k == e) & at_owner))
        def _():
            _drain(fin_dst.at[k], fin_recv.at[k])

        return carry

    lax.fori_loop(0, E, await_final, 0)
    for j in range(2):
        arrived = fin_dst[:, :, j * half_n : (j + 1) * half_n].reshape(nslot, half_n)
        for part in range(2):
            begin = part * half + j * half_n
            out[:, begin : begin + half_n] = _dot(places[part], arrived, ((0,), (0,))).astype(BF16)

    for h in range(2):
        _drain(stok.at[h, peers], tok_send.at[h])
        for k in range(3):
            _drain(rows.at[h, 0], row_send.at[h, k])
            _drain(rows.at[h, 0], fwd_send.at[h, k])
        _drain(rows.at[h, 0], hop_send.at[h])
    _drain(wstep_all.at[pl.ds(0, C - 1)], step_send)
    _drain(sss.at[peers], ss_send)
    _drain(ss.at[pl.ds(0, C - 1)], pos_send)
    for chip in range(chips):
        _drain(sback.at[chip, peers], back_send.at[chip])
    for bp in range(chips):
        _drain(gathered.at[bp, pl.ds(0, C - 1)], gated_send.at[bp])

    def left_final(k, carry):
        bp, q = k // (2 * group), lax.rem(k, 2 * group)

        @pl.when(jnp.logical_not((c * group + q // 2 == e) & (2 * bp + lax.rem(q, 2) == c)))
        def _():
            _drain(fin_src.at[bp, q], fin_send.at[k])

        return carry

    lax.fori_loop(0, E, left_final, 0)
    for k, where in enumerate((first_part, first_part, last_part, last_part, all_parts) + hops + (all_parts,) * 2 + (next_part,) * 2):
        _drain(w_out.at[0, where], wout_send.at[k])
    for k in range(2):
        _drain(w_out.at[0, hops[k]], across_send.at[k])


def per_device(
    tokens,
    route,
    w_inner,
    w_state,
    w_step,
    step_bias,
    decay_log,
    skip_gain,
    conv_weight,
    conv_bias,
    w_out,
):
    T, width = tokens.shape[1:]
    E, C = lax.axis_size("expert"), lax.axis_size("context")
    chips = C // 2
    chans = w_inner.shape[3]
    wide = w_state.shape[2] + C * 16
    vmem = pl.BlockSpec(memory_space=pltpu.VMEM)
    hbm = pl.BlockSpec(memory_space=pl.ANY)
    dma = pltpu.SemaphoreType.DMA
    flat = pltpu.VMEM((chips, E, 16, chans), BF16)
    mixed = pl.pallas_call(
        functools.partial(layer_kernel, E, C),
        out_shape=jax.ShapeDtypeStruct((T, width), BF16),
        in_specs=[vmem, vmem, hbm, vmem, vmem, vmem, vmem, vmem, vmem, vmem, hbm],
        out_specs=vmem,
        scratch_shapes=[
            pltpu.VMEM((C, T), jnp.int32),
            pltpu.VMEM((2, width // 4, 2, chans), BF16),
            pltpu.VMEM((2, width, chans), BF16),
            pltpu.VMEM((C, chans, width), BF16),
            pltpu.VMEM((2, E, 16, width // 4), BF16),
            pltpu.VMEM((2, E, 16, width // 4), BF16),
            pltpu.VMEM((2, C, E * 8, width // 2), BF16),
            flat,
            flat,
            flat,
            flat,
            flat,
            pltpu.VMEM((C, 16, width), BF16),
            pltpu.VMEM((E, 16, wide // 2), BF16),
            pltpu.VMEM((E, 16, wide // 2), BF16),
            pltpu.VMEM((C, T, wide), BF16),
            pltpu.VMEM((chips, C, E // C, 16, chans), BF16),
            pltpu.VMEM((chips, 2 * (E // C), 16, width // 2), BF16),
            pltpu.VMEM((E, 16, width // 2), BF16),
            pltpu.VMEM((HEAD_DIM, chans), F32),
            pltpu.VMEM((8, chans), F32),
            pltpu.VMEM((2, T, chans), BF16),
            dma((2,)),
            dma,
            dma((2,)),
            dma((2,)),
            dma,
            dma,
            dma((2, 3)),
            dma((2, C)),
            dma((2, 3)),
            dma((2,)),
            dma,
            dma,
            dma,
            dma,
            dma((chips,)),
            dma((chips,)),
            dma((11,)),
            dma((6, C)),
            dma((2,)),
            dma((chips,)),
            dma((chips,)),
            dma((chips,)),
            dma((chips,)),
            dma((E,)),
            dma((E,)),
        ],
        compiler_params=pltpu.CompilerParams(
            collective_id=0, has_side_effects=True, vmem_limit_bytes=VMEM_LIMIT
        ),
        name="layer",
    )(
        route[0, :, 0].reshape(C, T),
        tokens[0],
        w_inner[0],
        w_state[0],
        w_step[0].T,
        step_bias[None, :],
        decay_log[None, :],
        skip_gain[None, :],
        conv_weight,
        conv_bias[None, :],
        w_out[0],
    )
    return mixed[None]


def solution(mesh):
    in_specs = (
        P("expert", "context", None),
        P("expert", None, None),
        P("expert", None, None, "context"),
        P("expert", None, None),
        P("expert", None, "context"),
        P("context"),
        P("context"),
        P("context"),
        P(None, "context"),
        P("context"),
        P("expert", "context", None),
    )
    out_specs = P("expert", "context", None)
    return jax.shard_map(
        per_device, mesh=mesh, in_specs=in_specs, out_specs=out_specs, check_vma=False
    )
```

```python
import functools

import jax
import jax.numpy as jnp
from jax import lax
from jax.experimental import pallas as pl
from jax.experimental.pallas import tpu as pltpu
from jax.sharding import PartitionSpec as P

HEAD_DIM = 64
MESH = pl.DeviceIdType.MESH
F32 = jnp.float32
BF16 = jnp.bfloat16
VMEM_LIMIT = 60 * 1024 * 1024


def _dot(a, b, dims=((1,), (0,)), precision=None):
    return lax.dot_general(a, b, (dims, ((), ())), precision=precision, preferred_element_type=F32)


def _owner(seq, expert, E, C):
    return lax.rem(seq // (E // C) + expert, C)


def _greet(expert_peers, context_peers):
    e, c = lax.axis_index("expert"), lax.axis_index("context")
    barrier = pltpu.get_barrier_semaphore()

    def greet(axis, me, count):
        def body(k, carry):
            peer = lax.rem(me + k, count)
            pl.semaphore_signal(barrier, inc=1, device_id={axis: peer}, device_id_type=MESH)
            return carry

        lax.fori_loop(1, count, body, 0)

    greet("expert", e, expert_peers)
    greet("context", c, context_peers)

    def greet_owner(k, carry):
        owner = _owner(e, k, expert_peers, context_peers)

        @pl.when((k != e) | (owner != c))
        def _():
            pl.semaphore_signal(
                barrier, inc=1, device_id={"expert": k, "context": owner}, device_id_type=MESH
            )

        return carry

    lax.fori_loop(0, expert_peers, greet_owner, 0)


def _meet(expert_peers, context_peers):
    e, c = lax.axis_index("expert"), lax.axis_index("context")
    own = jnp.where(_owner(e, e, expert_peers, context_peers) == c, 1, 0)
    pl.semaphore_wait(pltpu.get_barrier_semaphore(), 2 * expert_peers + context_peers - 2 - own)


def _drain(ref, sem):
    pltpu.make_async_copy(ref, ref, sem).wait()


def _fold(top, bottom):
    n, w = top.shape[0] // 8, top.shape[1]
    return jnp.concatenate([top.reshape(n, 8, w), bottom.reshape(n, 8, w)], axis=1).astype(BF16)


def _unfold(folded):
    n, _, w = folded.shape
    wide = folded.astype(F32)
    return (
        wide[:, :8, :].reshape(n * 8, w).astype(BF16),
        wide[:, 8:, :].reshape(n * 8, w).astype(BF16),
    )


def _scatter_expert(E, src, dst, send_sem, recv_sem):
    e = lax.axis_index("expert")

    def body(k, carry):
        peer = lax.rem(e + k, E)
        pltpu.make_async_remote_copy(
            src_ref=src.at[peer],
            dst_ref=dst.at[e],
            send_sem=send_sem,
            recv_sem=recv_sem,
            device_id={"expert": peer},
            device_id_type=MESH,
        ).start()
        return carry

    lax.fori_loop(1, E, body, 0)
    dst[e] = src[e]


def _slot_onehot(row, n, half):
    place = row + (row & -8) + 8 * half
    return (lax.broadcasted_iota(jnp.int32, (n, row.shape[1]), 0) == place).astype(BF16)


def _remote(src, dst, send_sem, recv_sem, **where):
    return pltpu.make_async_remote_copy(
        src_ref=src,
        dst_ref=dst,
        send_sem=send_sem,
        recv_sem=recv_sem,
        device_id=where,
        device_id_type=MESH,
    )


def _softplus(v):
    return jnp.maximum(v, 0.0) + jnp.log1p(jnp.exp(-jnp.abs(v)))


def _iota(shape, axis):
    return lax.broadcasted_iota(jnp.int32, shape, axis)


def layer_kernel(
    E,
    C,
    ids,
    tokens,
    w_inner_hbm,
    w_state,
    w_step,
    step_bias,
    decay_log,
    skip_gain,
    conv_weight,
    conv_bias,
    w_out_hbm,
    out,
    slots,
    w3,
    w_inner,
    w_out,
    stok,
    rtok,
    rows,
    sinner,
    inner,
    gate,
    sback,
    back,
    wstep_all,
    sss,
    rss,
    ss,
    gathered,
    fin_src,
    fin_dst,
    state,
    tail8,
    scanned,
    w3_sem,
    w_sem,
    tok_send,
    tok_recv,
    step_send,
    step_recv,
    row_send,
    row_recv,
    fwd_send,
    hop_send,
    ss_send,
    ss_recv,
    pos_send,
    pos_recv,
    inner_send,
    inner_recv,
    wout_send,
    wout_recv,
    across_send,
    back_send,
    back_recv,
    gated_send,
    gated_recv,
    fin_send,
    fin_recv,
):
    e, c = lax.axis_index("expert"), lax.axis_index("context")
    x, core = c // 2, lax.rem(c, 2)
    sibling = c + 1 - 2 * core
    chips = C // 2
    T, width = tokens.shape
    half = width // 2
    quarter = width // 4
    chans = inner.shape[3]
    nrow = E * 8
    nslot = E * 16
    heads = w_step.shape[0]
    pieces, piece = w3.shape[0], w3.shape[1]
    count = width // piece
    depth = w_out.shape[1]
    early = depth // 16 * 4
    peers = pl.ds(0, E - 1)

    def load_piece(q):
        return pltpu.make_async_copy(
            w_inner_hbm.at[pl.ds(q * piece, piece)], w3.at[q % pieces], w3_sem.at[q % pieces]
        )

    _greet(E, C)
    for q in range(pieces):
        load_piece(q).start()
    load_w_out = pltpu.make_async_copy(w_out_hbm, w_out.at[c], w_sem)
    load_w_out.start()

    values = ids[...].astype(F32)
    eye = (_iota((T, T), 0) == _iota((T, T), 1)).astype(BF16)
    columns = _dot(eye, values.astype(BF16), ((1,), (1,)))
    earlier = _iota((T, T), 0) < _iota((T, T), 1)
    for b in range(C):
        same = (columns[:, b : b + 1] == values[b : b + 1, :]) & earlier
        rank = jnp.sum(same.astype(F32), axis=0, keepdims=True)
        slots[b : b + 1, :] = ids[b : b + 1, :] * 8 + rank.astype(jnp.int32)

    row = slots[pl.ds(c, 1), :]
    dispatch = (_iota((nrow, T), 0) == row).astype(BF16)

    def pack(h):
        a = h * half
        stok[h] = _fold(
            _dot(dispatch, tokens[:, a : a + quarter]),
            _dot(dispatch, tokens[:, a + quarter : a + half]),
        )

    pack(0)
    _meet(E, C)
    _scatter_expert(E, stok.at[0], rtok.at[0], tok_send.at[0], tok_recv.at[0])
    pack(1)
    _scatter_expert(E, stok.at[1], rtok.at[1], tok_send.at[1], tok_recv.at[1])

    def share(ref, send_sem, recv_sem):
        def body(k, carry):
            peer = lax.rem(c + k, C)
            _remote(ref.at[c], ref.at[c], send_sem, recv_sem, context=peer).start()
            return carry

        lax.fori_loop(1, C, body, 0)

    wide = w_step[...].astype(F32)
    wstep_all[c] = jnp.concatenate([wide, jnp.zeros((16 - heads, width), F32)], axis=0).astype(BF16)
    share(wstep_all, step_send, step_recv)

    right = lax.rem(x + 1, chips) * 2 + core
    left = lax.rem(x + chips - 1, chips) * 2 + core
    across = lax.rem(x + chips // 2, chips) * 2 + core

    def send_w_out(block, where, target, sem, kind):
        return _remote(
            w_out.at[block, where], w_out.at[block, where], sem, wout_recv.at[kind, block], context=target
        )

    def await_w_out(block, where, kind):
        _drain(w_out.at[block, where], wout_recv.at[kind, block])

    first_part, next_part = pl.ds(0, early), pl.ds(early, depth // 2 - early)
    last_part, all_parts = pl.ds(depth // 2, depth // 2), pl.ds(0, depth)
    hops = (pl.ds(0, depth // 2), last_part)
    load_w_out.wait()
    send_w_out(c, first_part, right, wout_send.at[0], 0).start()
    send_w_out(c, first_part, left, wout_send.at[1], 0).start()

    for q in range(count):
        load_piece(q).wait()

        def part_w(i, carry):
            block = w3[q % pieces, pl.ds(i * 128, 128)]
            at = pl.ds(pl.multiple_of(q * piece + i * 128, 128), 128)
            w_inner[0, at, :] = block[:, 0, :]
            w_inner[1, at, :] = block[:, 1, :]
            return carry

        lax.fori_loop(0, piece // 128, part_w, 0)
        if q + pieces < count:
            load_piece(q + pieces).start()

    def send_rows(h, block, target, sem):
        return _remote(rows.at[h, block], rows.at[h, block], sem, row_recv.at[h, block], context=target)

    def await_rows(h, block):
        _drain(rows.at[h, block], row_recv.at[h, block])

    for h in range(2):
        _drain(rtok.at[h, peers], tok_recv.at[h])
        first_q, second_q = _unfold(rtok[h])
        rows[h, c, :, :quarter] = first_q
        rows[h, c, :, quarter:] = second_q
        send_rows(h, c, right, row_send.at[h, 0]).start()
        send_rows(h, c, left, row_send.at[h, 1]).start()
        send_rows(h, c, sibling, row_send.at[h, 2]).start()

    _drain(wstep_all.at[pl.ds(0, C - 1)], step_recv)
    states, steps = [], []
    for h in range(2):
        mine = rows[h, c]
        at = slice(h * half, (h + 1) * half)
        step_w = wstep_all[:, :, at].reshape(C * 16, half)
        states.append(_dot(mine, w_state[at, :]))
        steps.append(_dot(mine, step_w, ((1,), (1,))))
    sss[...] = _fold(states[0] + states[1], steps[0] + steps[1])
    _scatter_expert(E, sss, rss, ss_send, ss_recv)

    step_n = min(256, chans)

    def project(chip, which, dst):
        first = rows[0, pl.ds(chip * 2, 2)].reshape(2 * nrow, half)
        second = rows[1, pl.ds(chip * 2, 2)].reshape(2 * nrow, half)
        for n in range(chans // step_n):
            cols = slice(n * step_n, (n + 1) * step_n)
            res = _dot(first, w_inner[which, :half, cols]) + _dot(second, w_inner[which, half:, cols])
            dst[chip, :, :, cols] = _fold(res[:nrow], res[nrow:])

    def inner_chip(chip):
        for h in range(2):
            await_rows(h, chip * 2 + 1 - core)
        project(chip, 1, sinner)
        _scatter_expert(E, sinner.at[chip], inner.at[chip], inner_send.at[chip], inner_recv.at[chip])

    inner_chip(x)
    await_rows(0, left)
    send_rows(0, left, right, hop_send.at[0]).start()
    send_rows(0, left, sibling, fwd_send.at[0, 0]).start()
    await_rows(0, right)
    send_rows(0, right, sibling, fwd_send.at[0, 1]).start()
    await_rows(1, right)
    send_rows(1, right, left, hop_send.at[1]).start()
    send_rows(1, right, sibling, fwd_send.at[1, 1]).start()
    await_rows(1, left)
    send_rows(1, left, sibling, fwd_send.at[1, 0]).start()

    _drain(rss.at[peers], ss_recv)
    vectors = rss[...].reshape(nslot, rss.shape[2])
    at_state = _dot(_slot_onehot(row, nslot, 0), vectors, ((0,), (0,)))
    at_step = _dot(_slot_onehot(row, nslot, 1), vectors, ((0,), (0,)))
    ss[c] = jnp.concatenate([at_state, at_step], axis=1).astype(BF16)
    share(ss, pos_send, pos_recv)

    send_w_out(c, next_part, right, wout_send.at[9], 5).start()
    send_w_out(c, last_part, left, wout_send.at[3], 1).start()
    send_w_out(c, last_part, right, wout_send.at[2], 1).start()
    send_w_out(c, next_part, left, wout_send.at[10], 5).start()
    send_w_out(c, all_parts, sibling, wout_send.at[4], 2).start()

    second = 1 - lax.rem(x, 2)
    third = jnp.where(x < 2, 2, x - 2)

    def other_chip(i, carry):
        chip = jnp.where(i == 0, second, jnp.where(i == 1, third, 6 - x - second - third))

        @pl.when(i == 1)
        def _():
            for h in range(2):
                await_rows(h, across)
                send_rows(h, across, sibling, fwd_send.at[h, 2]).start()

        inner_chip(chip)
        return carry

    lax.fori_loop(0, chips - 1, other_chip, 0)

    def gate_chip(chip, carry):
        project(chip, 0, gate)
        return carry

    lax.fori_loop(0, chips, gate_chip, 0)

    exact = lax.Precision.HIGHEST
    taps = conv_weight.shape[0]
    nbc = HEAD_DIM
    state[...] = jnp.zeros_like(state)
    tail8[...] = jnp.zeros_like(tail8)
    lower = _iota((T, T), 0) >= _iota((T, T), 1)
    lower_one = lower.astype(F32)
    upper_one = (_iota((T, T), 0) <= _iota((T, T), 1)).astype(F32)
    first = _iota((T, 2 * HEAD_DIM), 1) < HEAD_DIM
    lanes = C * 16
    pick = (_iota((lanes, heads), 0) == c * 16 + _iota((lanes, heads), 1)).astype(BF16)
    pick_t = (_iota((heads, lanes), 1) == c * 16 + _iota((heads, lanes), 0)).astype(BF16)
    diagonal = _iota((heads, heads), 0) == _iota((heads, heads), 1)

    def column(v):
        return jnp.sum(jnp.where(diagonal, v, 0.0), axis=1, keepdims=True)

    bias_l, rate_l = step_bias[...], -jnp.exp(decay_log[...])
    bias_r, rate_r = column(bias_l), column(rate_l)
    gain = skip_gain[...]

    def chunk(b, part):
        place = _slot_onehot(slots[pl.ds(b, 1), :], nslot, part)
        raw = _dot(place, inner[b // 2].reshape(nslot, chans), ((0,), (0,)))
        joined = jnp.concatenate([tail8[...], raw], axis=0)
        tail8[...] = raw[T - 8 :, :]
        conv = conv_bias[...] + jnp.zeros_like(raw)
        for j in range(taps):
            begin = 8 - taps + 1 + j
            conv = conv + conv_weight[j : j + 1, :] * joined[begin : begin + T, :]
        signal = conv * jax.nn.sigmoid(conv)

        mine = ss[b]
        keys, queries = mine[:, :nbc], mine[:, nbc : 2 * nbc]
        raw_step = mine[:, 2 * nbc :]
        steps = _softplus(_dot(raw_step, pick) + bias_l)
        steps_t = _softplus(_dot(pick_t, raw_step, ((1,), (1,))) + bias_r)
        summed = _dot(lower_one, steps * rate_l, precision=exact)
        summed_t = _dot(steps_t * rate_r, upper_one, precision=exact)
        scores = _dot(queries, keys, ((1,), (1,)))
        grown = jnp.exp(summed)
        end = summed[T - 1 : T, :]
        tail = jnp.exp(end - summed) * steps
        whole = jnp.exp(end)
        for pair in range(heads // 2):
            cols = slice(pair * 2 * HEAD_DIM, (pair + 1) * 2 * HEAD_DIM)
            xs = signal[:, cols]
            xb = xs.astype(BF16)
            weights = []
            for h in (2 * pair, 2 * pair + 1):
                gaps = summed[:, h : h + 1] - summed_t[h : h + 1, :]
                decay = jnp.exp(jnp.where(lower, gaps, -jnp.inf))
                weights.append((scores * decay * steps_t[h : h + 1, :]).astype(BF16))
            zero = jnp.zeros_like(xb)
            stacked = jnp.concatenate([jnp.where(first, xb, zero), jnp.where(first, zero, xb)], axis=0)
            local = _dot(jnp.concatenate(weights, axis=1), stacked)

            def spread(v):
                n = v.shape[0]
                a = jnp.broadcast_to(v[:, 2 * pair : 2 * pair + 1], (n, 2 * HEAD_DIM))
                z = jnp.broadcast_to(v[:, 2 * pair + 1 : 2 * pair + 2], (n, 2 * HEAD_DIM))
                return jnp.where(first[:n], a, z)

            old = state[:, cols]
            carried = spread(grown) * _dot(queries, old.astype(BF16))
            fed = (spread(tail) * xs).astype(BF16)
            state[:, cols] = spread(whole) * old + _dot(keys, fed, ((0,), (0,)))
            scanned[part, :, cols] = (local + carried + spread(gain) * xs).astype(BF16)

    _drain(ss.at[pl.ds(0, C - 1)], pos_recv)

    def pair_of_chunks(bp, carry):
        _drain(inner.at[bp, peers], inner_recv.at[bp])

        @pl.when(bp == chips - 1)
        def _():
            await_w_out(left, first_part, 0)
            await_w_out(left, next_part, 5)
            send_w_out(left, hops[0], right, wout_send.at[5], 3).start()
            await_w_out(right, last_part, 1)
            send_w_out(right, hops[1], left, wout_send.at[6], 4).start()

        chunk(2 * bp, 0)
        chunk(2 * bp + 1, 1)
        total = None
        for part in range(2):
            place = _slot_onehot(slots[pl.ds(2 * bp + part, 1), :], nslot, part)
            term = _dot(place, scanned[part])
            total = term if total is None else total + term
        sback[bp] = total.astype(BF16).reshape(E, 16, chans)
        _scatter_expert(E, sback.at[bp], back.at[bp], back_send.at[bp], back_recv.at[bp])

        return carry

    lax.fori_loop(0, chips, pair_of_chunks, 0)

    for chip in range(chips):
        _drain(sinner.at[chip, peers], inner_send.at[chip])

    group = E // C

    def first_of(owner):
        return lax.rem(owner + C - lax.rem(e, C), C) * group

    def gate_rows(bp, carry):
        _drain(back.at[bp, peers], back_recv.at[bp])
        g = gate[bp].astype(F32)
        v = back[bp].astype(F32) * (g * jax.nn.sigmoid(g))
        sinner[bp] = v.astype(BF16)

        def send(k, carry):
            target = lax.rem(c + k, C)
            _remote(
                sinner.at[bp, pl.ds(first_of(target), group)],
                gathered.at[bp, c],
                gated_send.at[bp],
                gated_recv.at[bp],
                context=target,
            ).start()
            return carry

        lax.fori_loop(1, C, send, 0)
        gathered[bp, c] = sinner[bp, pl.ds(first_of(c), group)]
        return carry

    half_n = half // 2

    def multiply(begin, end):
        for bp in range(begin, end):
            _drain(gathered.at[bp, pl.ds(0, C - 1)], gated_recv.at[bp])
        count_rows = (end - begin) * group * 16

        def columns_of(j, carry):
            sums = []
            for late in range(2):
                total = jnp.zeros((count_rows, half_n), F32)
                cols = pl.ds(pl.multiple_of(late * half + j * half_n, half_n), half_n)
                for block in range(C):
                    mine = gathered[begin:end, block].reshape(count_rows, chans)
                    total = total + _dot(mine, w_out[block, :, cols])
                sums.append(total)
            at = pl.ds(pl.multiple_of(j * half_n, half_n), half_n)
            folded = _fold(*sums).reshape(end - begin, 2 * group, 16, half_n)
            fin_src[begin:end, :, :, at] = folded
            return carry

        lax.fori_loop(0, 2, columns_of, 0)

    def send_final(begin, end):
        def send(k, carry):
            q, bp = k // (end - begin), begin + lax.rem(k + x, end - begin)
            seq, block = first_of(c) + q // 2, 2 * bp + lax.rem(q, 2)
            here = (seq == e) & (block == c)

            @pl.when(jnp.logical_not(here))
            def _():
                _remote(
                    fin_src.at[bp, q],
                    fin_dst.at[e],
                    fin_send.at[bp * 2 * group + q],
                    fin_recv.at[e],
                    expert=seq,
                    context=block,
                ).start()

            @pl.when(here)
            def _():
                fin_dst[e] = fin_src[bp, q]

            return carry

        lax.fori_loop(0, (end - begin) * 2 * group, send, 0)

    await_w_out(right, first_part, 0)
    await_w_out(right, next_part, 5)
    send_w_out(right, all_parts, sibling, wout_send.at[8], 2).start()
    await_w_out(left, last_part, 1)
    send_w_out(left, all_parts, sibling, wout_send.at[7], 2).start()
    lax.fori_loop(0, chips - 1, gate_rows, 0)
    for k in range(2):
        await_w_out(across, hops[k], 3 + k)
        send_w_out(across, hops[k], sibling, across_send.at[k], 3 + k).start()
    gate_rows(chips - 1, 0)
    for block in (sibling, left + 1 - 2 * core, right + 1 - 2 * core):
        await_w_out(block, all_parts, 2)
    for k in range(2):
        await_w_out(across + 1 - 2 * core, hops[k], 3 + k)
    multiply(0, chips // 2)
    send_final(0, chips // 2)
    for bp in range(chips // 2, chips):
        multiply(bp, bp + 1)
        send_final(bp, bp + 1)

    places = [
        _dot(eye, _slot_onehot(row, nslot, part), ((1,), (1,))).astype(BF16) for part in range(2)
    ]
    at_owner = c == _owner(e, e, E, C)

    def await_final(k, carry):
        @pl.when(jnp.logical_not((k == e) & at_owner))
        def _():
            _drain(fin_dst.at[k], fin_recv.at[k])

        return carry

    lax.fori_loop(0, E, await_final, 0)
    for j in range(2):
        arrived = fin_dst[:, :, j * half_n : (j + 1) * half_n].reshape(nslot, half_n)
        for part in range(2):
            begin = part * half + j * half_n
            out[:, begin : begin + half_n] = _dot(places[part], arrived).astype(BF16)

    for h in range(2):
        _drain(stok.at[h, peers], tok_send.at[h])
        for k in range(3):
            _drain(rows.at[h, 0], row_send.at[h, k])
            _drain(rows.at[h, 0], fwd_send.at[h, k])
        _drain(rows.at[h, 0], hop_send.at[h])
    _drain(wstep_all.at[pl.ds(0, C - 1)], step_send)
    _drain(sss.at[peers], ss_send)
    _drain(ss.at[pl.ds(0, C - 1)], pos_send)
    for chip in range(chips):
        _drain(sback.at[chip, peers], back_send.at[chip])
    for bp in range(chips):
        _drain(gathered.at[bp, pl.ds(0, C - 1)], gated_send.at[bp])

    def left_final(k, carry):
        bp, q = k // (2 * group), lax.rem(k, 2 * group)

        @pl.when(jnp.logical_not((first_of(c) + q // 2 == e) & (2 * bp + lax.rem(q, 2) == c)))
        def _():
            _drain(fin_src.at[bp, q], fin_send.at[k])

        return carry

    lax.fori_loop(0, E, left_final, 0)
    for k, where in enumerate((first_part, first_part, last_part, last_part, all_parts) + hops + (all_parts,) * 2 + (next_part,) * 2):
        _drain(w_out.at[0, where], wout_send.at[k])
    for k in range(2):
        _drain(w_out.at[0, hops[k]], across_send.at[k])


def per_device(
    tokens,
    route,
    w_inner,
    w_state,
    w_step,
    step_bias,
    decay_log,
    skip_gain,
    conv_weight,
    conv_bias,
    w_out,
):
    T, width = tokens.shape[1:]
    E, C = lax.axis_size("expert"), lax.axis_size("context")
    chips = C // 2
    chans = w_inner.shape[3]
    wide = w_state.shape[2] + C * 16
    vmem = pl.BlockSpec(memory_space=pltpu.VMEM)
    hbm = pl.BlockSpec(memory_space=pl.ANY)
    dma = pltpu.SemaphoreType.DMA
    flat = pltpu.VMEM((chips, E, 16, chans), BF16)
    mixed = pl.pallas_call(
        functools.partial(layer_kernel, E, C),
        out_shape=jax.ShapeDtypeStruct((T, width), BF16),
        in_specs=[vmem, vmem, hbm, vmem, vmem, vmem, vmem, vmem, vmem, vmem, hbm],
        out_specs=vmem,
        scratch_shapes=[
            pltpu.VMEM((C, T), jnp.int32),
            pltpu.VMEM((2, width // 4, 2, chans), BF16),
            pltpu.VMEM((2, width, chans), BF16),
            pltpu.VMEM((C, chans, width), BF16),
            pltpu.VMEM((2, E, 16, width // 4), BF16),
            pltpu.VMEM((2, E, 16, width // 4), BF16),
            pltpu.VMEM((2, C, E * 8, width // 2), BF16),
            flat,
            flat,
            flat,
            flat,
            flat,
            pltpu.VMEM((C, 16, width), BF16),
            pltpu.VMEM((E, 16, wide // 2), BF16),
            pltpu.VMEM((E, 16, wide // 2), BF16),
            pltpu.VMEM((C, T, wide), BF16),
            pltpu.VMEM((chips, C, E // C, 16, chans), BF16),
            pltpu.VMEM((chips, 2 * (E // C), 16, width // 2), BF16),
            pltpu.VMEM((E, 16, width // 2), BF16),
            pltpu.VMEM((HEAD_DIM, chans), F32),
            pltpu.VMEM((8, chans), F32),
            pltpu.VMEM((2, T, chans), BF16),
            dma((2,)),
            dma,
            dma((2,)),
            dma((2,)),
            dma,
            dma,
            dma((2, 3)),
            dma((2, C)),
            dma((2, 3)),
            dma((2,)),
            dma,
            dma,
            dma,
            dma,
            dma((chips,)),
            dma((chips,)),
            dma((11,)),
            dma((6, C)),
            dma((2,)),
            dma((chips,)),
            dma((chips,)),
            dma((chips,)),
            dma((chips,)),
            dma((E,)),
            dma((E,)),
        ],
        compiler_params=pltpu.CompilerParams(
            collective_id=0, has_side_effects=True, vmem_limit_bytes=VMEM_LIMIT
        ),
        name="layer",
    )(
        route[0, :, 0].reshape(C, T),
        tokens[0],
        w_inner[0],
        w_state[0],
        w_step[0].T,
        step_bias[None, :],
        decay_log[None, :],
        skip_gain[None, :],
        conv_weight,
        conv_bias[None, :],
        w_out[0],
    )
    return mixed[None]


def solution(mesh):
    in_specs = (
        P("expert", "context", None),
        P("expert", None, None),
        P("expert", None, None, "context"),
        P("expert", None, None),
        P("expert", None, "context"),
        P("context"),
        P("context"),
        P("context"),
        P(None, "context"),
        P("context"),
        P("expert", "context", None),
    )
    out_specs = P("expert", "context", None)
    return jax.shard_map(
        per_device, mesh=mesh, in_specs=in_specs, out_specs=out_specs, check_vma=False
    )
```

```python
import functools

import jax
import jax.numpy as jnp
from jax import lax
from jax.experimental import pallas as pl
from jax.experimental.pallas import tpu as pltpu
from jax.sharding import PartitionSpec as P

HEAD_DIM = 64
MESH = pl.DeviceIdType.MESH
F32 = jnp.float32
BF16 = jnp.bfloat16
VMEM_LIMIT = 60 * 1024 * 1024


def _dot(a, b, dims=((1,), (0,)), precision=None):
    return lax.dot_general(a, b, (dims, ((), ())), precision=precision, preferred_element_type=F32)


def _owner(seq, expert, E, C):
    return lax.rem(seq // (E // C) + expert, C)


def _greet(expert_peers, context_peers):
    e, c = lax.axis_index("expert"), lax.axis_index("context")
    barrier = pltpu.get_barrier_semaphore()

    def greet(axis, me, count):
        def body(k, carry):
            peer = lax.rem(me + k, count)
            pl.semaphore_signal(barrier, inc=1, device_id={axis: peer}, device_id_type=MESH)
            return carry

        lax.fori_loop(1, count, body, 0)

    greet("expert", e, expert_peers)
    greet("context", c, context_peers)

    def greet_owner(k, carry):
        owner = _owner(e, k, expert_peers, context_peers)

        @pl.when((k != e) | (owner != c))
        def _():
            pl.semaphore_signal(
                barrier, inc=1, device_id={"expert": k, "context": owner}, device_id_type=MESH
            )

        return carry

    lax.fori_loop(0, expert_peers, greet_owner, 0)


def _meet(expert_peers, context_peers):
    e, c = lax.axis_index("expert"), lax.axis_index("context")
    own = jnp.where(_owner(e, e, expert_peers, context_peers) == c, 1, 0)
    pl.semaphore_wait(pltpu.get_barrier_semaphore(), 2 * expert_peers + context_peers - 2 - own)


def _drain(ref, sem):
    pltpu.make_async_copy(ref, ref, sem).wait()


def _fold(top, bottom):
    n, w = top.shape[0] // 8, top.shape[1]
    return jnp.concatenate([top.reshape(n, 8, w), bottom.reshape(n, 8, w)], axis=1).astype(BF16)


def _unfold(folded):
    n, _, w = folded.shape
    wide = folded.astype(F32)
    return (
        wide[:, :8, :].reshape(n * 8, w).astype(BF16),
        wide[:, 8:, :].reshape(n * 8, w).astype(BF16),
    )


def _scatter_expert(E, src, dst, send_sem, recv_sem):
    e = lax.axis_index("expert")

    def body(k, carry):
        peer = lax.rem(e + k, E)
        pltpu.make_async_remote_copy(
            src_ref=src.at[peer],
            dst_ref=dst.at[e],
            send_sem=send_sem,
            recv_sem=recv_sem,
            device_id={"expert": peer},
            device_id_type=MESH,
        ).start()
        return carry

    lax.fori_loop(1, E, body, 0)
    dst[e] = src[e]


def _slot_onehot(row, n, half):
    place = row + (row & -8) + 8 * half
    return (lax.broadcasted_iota(jnp.int32, (n, row.shape[1]), 0) == place).astype(BF16)


def _remote(src, dst, send_sem, recv_sem, **where):
    return pltpu.make_async_remote_copy(
        src_ref=src,
        dst_ref=dst,
        send_sem=send_sem,
        recv_sem=recv_sem,
        device_id=where,
        device_id_type=MESH,
    )


def _softplus(v):
    return jnp.maximum(v, 0.0) + jnp.log1p(jnp.exp(-jnp.abs(v)))


def _iota(shape, axis):
    return lax.broadcasted_iota(jnp.int32, shape, axis)


def layer_kernel(
    E,
    C,
    ids,
    tokens_hbm,
    w_inner_hbm,
    w_state_hbm,
    w_step,
    step_bias,
    decay_log,
    skip_gain,
    conv_weight,
    conv_bias,
    w_out_hbm,
    out,
    tokens,
    w_state,
    slots,
    w3,
    w_inner,
    w_out,
    stok,
    rtok,
    rows,
    sinner,
    inner,
    gate,
    sback,
    back,
    wstep_all,
    sss,
    rss,
    ss,
    gathered,
    fin_src,
    fin_dst,
    state,
    tail8,
    scanned,
    in_sem,
    w3_sem,
    w_sem,
    tok_send,
    tok_recv,
    step_send,
    step_recv,
    row_send,
    row_recv,
    fwd_send,
    hop_send,
    ss_send,
    ss_recv,
    pos_send,
    pos_recv,
    inner_send,
    inner_recv,
    wout_send,
    wout_recv,
    across_send,
    back_send,
    back_recv,
    gated_send,
    gated_recv,
    fin_send,
    fin_recv,
):
    e, c = lax.axis_index("expert"), lax.axis_index("context")
    x, core = c // 2, lax.rem(c, 2)
    sibling = c + 1 - 2 * core
    chips = C // 2
    T, width = tokens.shape
    half = width // 2
    quarter = width // 4
    chans = inner.shape[3]
    nrow = E * 8
    nslot = E * 16
    heads = w_step.shape[0]
    pieces, piece = w3.shape[0], w3.shape[1]
    count = width // piece
    depth = w_out.shape[1]
    early = depth // 16 * 4
    peers = pl.ds(0, E - 1)

    def load_piece(q):
        return pltpu.make_async_copy(
            w_inner_hbm.at[pl.ds(q * piece, piece)], w3.at[q % pieces], w3_sem.at[q % pieces]
        )

    _greet(E, C)
    load_tokens = pltpu.make_async_copy(tokens_hbm, tokens, in_sem.at[0])
    load_tokens.start()
    load_w_state = pltpu.make_async_copy(w_state_hbm, w_state, in_sem.at[1])
    load_w_state.start()
    for q in range(pieces):
        load_piece(q).start()
    load_w_out = pltpu.make_async_copy(w_out_hbm, w_out.at[c], w_sem)
    load_w_out.start()

    values = ids[...].astype(F32)
    eye = (_iota((T, T), 0) == _iota((T, T), 1)).astype(BF16)
    columns = _dot(eye, values.astype(BF16), ((1,), (1,)))
    earlier = _iota((T, T), 0) < _iota((T, T), 1)
    for b in range(C):
        same = (columns[:, b : b + 1] == values[b : b + 1, :]) & earlier
        rank = jnp.sum(same.astype(F32), axis=0, keepdims=True)
        slots[b : b + 1, :] = ids[b : b + 1, :] * 8 + rank.astype(jnp.int32)

    row = slots[pl.ds(c, 1), :]
    dispatch = (_iota((nrow, T), 0) == row).astype(BF16)

    def pack(h):
        a = h * half
        stok[h] = _fold(
            _dot(dispatch, tokens[:, a : a + quarter]),
            _dot(dispatch, tokens[:, a + quarter : a + half]),
        )

    load_tokens.wait()
    pack(0)
    _meet(E, C)
    _scatter_expert(E, stok.at[0], rtok.at[0], tok_send.at[0], tok_recv.at[0])
    pack(1)
    _scatter_expert(E, stok.at[1], rtok.at[1], tok_send.at[1], tok_recv.at[1])

    def share(ref, send_sem, recv_sem):
        def body(k, carry):
            peer = lax.rem(c + k, C)
            _remote(ref.at[c], ref.at[c], send_sem, recv_sem, context=peer).start()
            return carry

        lax.fori_loop(1, C, body, 0)

    wide = w_step[...].astype(F32)
    wstep_all[c] = jnp.concatenate([wide, jnp.zeros((16 - heads, width), F32)], axis=0).astype(BF16)
    share(wstep_all, step_send, step_recv)

    right = lax.rem(x + 1, chips) * 2 + core
    left = lax.rem(x + chips - 1, chips) * 2 + core
    across = lax.rem(x + chips // 2, chips) * 2 + core

    def send_w_out(block, where, target, sem, kind):
        return _remote(
            w_out.at[block, where], w_out.at[block, where], sem, wout_recv.at[kind, block], context=target
        )

    def await_w_out(block, where, kind):
        _drain(w_out.at[block, where], wout_recv.at[kind, block])

    first_part, next_part = pl.ds(0, early), pl.ds(early, depth // 2 - early)
    last_part, all_parts = pl.ds(depth // 2, depth // 2), pl.ds(0, depth)
    hops = (pl.ds(0, depth // 2), last_part)
    load_w_out.wait()
    send_w_out(c, first_part, right, wout_send.at[0], 0).start()
    send_w_out(c, first_part, left, wout_send.at[1], 0).start()

    for q in range(count):
        load_piece(q).wait()

        def part_w(i, carry):
            block = w3[q % pieces, pl.ds(i * 128, 128)]
            at = pl.ds(pl.multiple_of(q * piece + i * 128, 128), 128)
            w_inner[0, at, :] = block[:, 0, :]
            w_inner[1, at, :] = block[:, 1, :]
            return carry

        lax.fori_loop(0, piece // 128, part_w, 0)
        if q + pieces < count:
            load_piece(q + pieces).start()

    def send_rows(h, block, target, sem):
        return _remote(rows.at[h, block], rows.at[h, block], sem, row_recv.at[h, block], context=target)

    def await_rows(h, block):
        _drain(rows.at[h, block], row_recv.at[h, block])

    for h in range(2):
        _drain(rtok.at[h, peers], tok_recv.at[h])
        first_q, second_q = _unfold(rtok[h])
        rows[h, c, :, :quarter] = first_q
        rows[h, c, :, quarter:] = second_q
        send_rows(h, c, right, row_send.at[h, 0]).start()
        send_rows(h, c, left, row_send.at[h, 1]).start()
        send_rows(h, c, sibling, row_send.at[h, 2]).start()

    _drain(wstep_all.at[pl.ds(0, C - 1)], step_recv)
    load_w_state.wait()
    states, steps = [], []
    for h in range(2):
        mine = rows[h, c]
        at = slice(h * half, (h + 1) * half)
        step_w = wstep_all[:, :, at].reshape(C * 16, half)
        states.append(_dot(mine, w_state[at, :]))
        steps.append(_dot(mine, step_w, ((1,), (1,))))
    sss[...] = _fold(states[0] + states[1], steps[0] + steps[1])
    _scatter_expert(E, sss, rss, ss_send, ss_recv)

    step_n = min(256, chans)

    def project(chip, which, dst):
        first = rows[0, pl.ds(chip * 2, 2)].reshape(2 * nrow, half)
        second = rows[1, pl.ds(chip * 2, 2)].reshape(2 * nrow, half)
        for n in range(chans // step_n):
            cols = slice(n * step_n, (n + 1) * step_n)
            res = _dot(first, w_inner[which, :half, cols]) + _dot(second, w_inner[which, half:, cols])
            dst[chip, :, :, cols] = _fold(res[:nrow], res[nrow:])

    def inner_chip(chip):
        for h in range(2):
            await_rows(h, chip * 2 + 1 - core)
        project(chip, 1, sinner)
        _scatter_expert(E, sinner.at[chip], inner.at[chip], inner_send.at[chip], inner_recv.at[chip])

    inner_chip(x)
    await_rows(0, left)
    send_rows(0, left, right, hop_send.at[0]).start()
    send_rows(0, left, sibling, fwd_send.at[0, 0]).start()
    await_rows(0, right)
    send_rows(0, right, sibling, fwd_send.at[0, 1]).start()
    await_rows(1, right)
    send_rows(1, right, left, hop_send.at[1]).start()
    send_rows(1, right, sibling, fwd_send.at[1, 1]).start()
    await_rows(1, left)
    send_rows(1, left, sibling, fwd_send.at[1, 0]).start()

    _drain(rss.at[peers], ss_recv)
    vectors = rss[...].reshape(nslot, rss.shape[2])
    at_state = _dot(_slot_onehot(row, nslot, 0), vectors, ((0,), (0,)))
    at_step = _dot(_slot_onehot(row, nslot, 1), vectors, ((0,), (0,)))
    ss[c] = jnp.concatenate([at_state, at_step], axis=1).astype(BF16)
    share(ss, pos_send, pos_recv)

    send_w_out(c, next_part, right, wout_send.at[9], 5).start()
    send_w_out(c, last_part, left, wout_send.at[3], 1).start()
    send_w_out(c, last_part, right, wout_send.at[2], 1).start()
    send_w_out(c, next_part, left, wout_send.at[10], 5).start()
    send_w_out(c, all_parts, sibling, wout_send.at[4], 2).start()

    second = 1 - lax.rem(x, 2)
    third = jnp.where(x < 2, 2, x - 2)

    def other_chip(i, carry):
        chip = jnp.where(i == 0, second, jnp.where(i == 1, third, 6 - x - second - third))

        @pl.when(i == 1)
        def _():
            for h in range(2):
                await_rows(h, across)
                send_rows(h, across, sibling, fwd_send.at[h, 2]).start()

        inner_chip(chip)
        return carry

    lax.fori_loop(0, chips - 1, other_chip, 0)

    def gate_chip(chip, carry):
        project(chip, 0, gate)
        return carry

    lax.fori_loop(0, chips, gate_chip, 0)

    exact = lax.Precision.HIGHEST
    taps = conv_weight.shape[0]
    nbc = HEAD_DIM
    state[...] = jnp.zeros_like(state)
    tail8[...] = jnp.zeros_like(tail8)
    lower = _iota((T, T), 0) >= _iota((T, T), 1)
    lower_one = lower.astype(F32)
    upper_one = (_iota((T, T), 0) <= _iota((T, T), 1)).astype(F32)
    first = _iota((T, 2 * HEAD_DIM), 1) < HEAD_DIM
    lanes = C * 16
    pick = (_iota((lanes, heads), 0) == c * 16 + _iota((lanes, heads), 1)).astype(BF16)
    pick_t = (_iota((heads, lanes), 1) == c * 16 + _iota((heads, lanes), 0)).astype(BF16)
    diagonal = _iota((heads, heads), 0) == _iota((heads, heads), 1)

    def column(v):
        return jnp.sum(jnp.where(diagonal, v, 0.0), axis=1, keepdims=True)

    bias_l, rate_l = step_bias[...], -jnp.exp(decay_log[...])
    bias_r, rate_r = column(bias_l), column(rate_l)
    gain = skip_gain[...]

    def chunk(b, part):
        place = _slot_onehot(slots[pl.ds(b, 1), :], nslot, part)
        raw = _dot(place, inner[b // 2].reshape(nslot, chans), ((0,), (0,)))
        joined = jnp.concatenate([tail8[...], raw], axis=0)
        tail8[...] = raw[T - 8 :, :]
        conv = conv_bias[...] + jnp.zeros_like(raw)
        for j in range(taps):
            begin = 8 - taps + 1 + j
            conv = conv + conv_weight[j : j + 1, :] * joined[begin : begin + T, :]
        signal = conv * jax.nn.sigmoid(conv)

        mine = ss[b]
        keys, queries = mine[:, :nbc], mine[:, nbc : 2 * nbc]
        raw_step = mine[:, 2 * nbc :]
        steps = _softplus(_dot(raw_step, pick) + bias_l)
        steps_t = _softplus(_dot(pick_t, raw_step, ((1,), (1,))) + bias_r)
        summed = _dot(lower_one, steps * rate_l, precision=exact)
        summed_t = _dot(steps_t * rate_r, upper_one, precision=exact)
        scores = _dot(queries, keys, ((1,), (1,)))
        grown = jnp.exp(summed)
        end = summed[T - 1 : T, :]
        tail = jnp.exp(end - summed) * steps
        whole = jnp.exp(end)
        for pair in range(heads // 2):
            cols = slice(pair * 2 * HEAD_DIM, (pair + 1) * 2 * HEAD_DIM)
            xs = signal[:, cols]
            xb = xs.astype(BF16)
            weights = []
            for h in (2 * pair, 2 * pair + 1):
                gaps = summed[:, h : h + 1] - summed_t[h : h + 1, :]
                decay = jnp.exp(jnp.where(lower, gaps, -jnp.inf))
                weights.append((scores * decay * steps_t[h : h + 1, :]).astype(BF16))
            zero = jnp.zeros_like(xb)
            stacked = jnp.concatenate([jnp.where(first, xb, zero), jnp.where(first, zero, xb)], axis=0)
            local = _dot(jnp.concatenate(weights, axis=1), stacked)

            def spread(v):
                n = v.shape[0]
                a = jnp.broadcast_to(v[:, 2 * pair : 2 * pair + 1], (n, 2 * HEAD_DIM))
                z = jnp.broadcast_to(v[:, 2 * pair + 1 : 2 * pair + 2], (n, 2 * HEAD_DIM))
                return jnp.where(first[:n], a, z)

            old = state[:, cols]
            carried = spread(grown) * _dot(queries, old.astype(BF16))
            fed = (spread(tail) * xs).astype(BF16)
            state[:, cols] = spread(whole) * old + _dot(keys, fed, ((0,), (0,)))
            scanned[part, :, cols] = (local + carried + spread(gain) * xs).astype(BF16)

    _drain(ss.at[pl.ds(0, C - 1)], pos_recv)

    def pair_of_chunks(bp, carry):
        _drain(inner.at[bp, peers], inner_recv.at[bp])

        @pl.when(bp == chips - 1)
        def _():
            await_w_out(left, first_part, 0)
            await_w_out(left, next_part, 5)
            send_w_out(left, hops[0], right, wout_send.at[5], 3).start()
            await_w_out(right, last_part, 1)
            send_w_out(right, hops[1], left, wout_send.at[6], 4).start()

        chunk(2 * bp, 0)
        chunk(2 * bp + 1, 1)
        total = None
        for part in range(2):
            place = _slot_onehot(slots[pl.ds(2 * bp + part, 1), :], nslot, part)
            term = _dot(place, scanned[part])
            total = term if total is None else total + term
        sback[bp] = total.astype(BF16).reshape(E, 16, chans)
        _scatter_expert(E, sback.at[bp], back.at[bp], back_send.at[bp], back_recv.at[bp])

        return carry

    lax.fori_loop(0, chips, pair_of_chunks, 0)

    for chip in range(chips):
        _drain(sinner.at[chip, peers], inner_send.at[chip])

    group = E // C

    def first_of(owner):
        return lax.rem(owner + C - lax.rem(e, C), C) * group

    def gate_rows(bp, carry):
        _drain(back.at[bp, peers], back_recv.at[bp])
        g = gate[bp].astype(F32)
        v = back[bp].astype(F32) * (g * jax.nn.sigmoid(g))
        sinner[bp] = v.astype(BF16)

        def send(k, carry):
            target = lax.rem(c + k, C)
            _remote(
                sinner.at[bp, pl.ds(first_of(target), group)],
                gathered.at[bp, c],
                gated_send.at[bp],
                gated_recv.at[bp],
                context=target,
            ).start()
            return carry

        lax.fori_loop(1, C, send, 0)
        gathered[bp, c] = sinner[bp, pl.ds(first_of(c), group)]
        return carry

    half_n = half // 2

    def multiply(begin, end):
        for bp in range(begin, end):
            _drain(gathered.at[bp, pl.ds(0, C - 1)], gated_recv.at[bp])
        count_rows = (end - begin) * group * 16

        def columns_of(j, carry):
            sums = []
            for late in range(2):
                total = jnp.zeros((count_rows, half_n), F32)
                cols = pl.ds(pl.multiple_of(late * half + j * half_n, half_n), half_n)
                for block in range(C):
                    mine = gathered[begin:end, block].reshape(count_rows, chans)
                    total = total + _dot(mine, w_out[block, :, cols])
                sums.append(total)
            at = pl.ds(pl.multiple_of(j * half_n, half_n), half_n)
            folded = _fold(*sums).reshape(end - begin, 2 * group, 16, half_n)
            fin_src[begin:end, :, :, at] = folded
            return carry

        lax.fori_loop(0, 2, columns_of, 0)

    def send_final(begin, end):
        def send(k, carry):
            q, bp = k // (end - begin), begin + lax.rem(k + x, end - begin)
            seq, block = first_of(c) + q // 2, 2 * bp + lax.rem(q, 2)
            here = (seq == e) & (block == c)

            @pl.when(jnp.logical_not(here))
            def _():
                _remote(
                    fin_src.at[bp, q],
                    fin_dst.at[e],
                    fin_send.at[bp * 2 * group + q],
                    fin_recv.at[e],
                    expert=seq,
                    context=block,
                ).start()

            @pl.when(here)
            def _():
                fin_dst[e] = fin_src[bp, q]

            return carry

        lax.fori_loop(0, (end - begin) * 2 * group, send, 0)

    await_w_out(right, first_part, 0)
    await_w_out(right, next_part, 5)
    send_w_out(right, all_parts, sibling, wout_send.at[8], 2).start()
    await_w_out(left, last_part, 1)
    send_w_out(left, all_parts, sibling, wout_send.at[7], 2).start()
    lax.fori_loop(0, chips - 1, gate_rows, 0)
    for k in range(2):
        await_w_out(across, hops[k], 3 + k)
        send_w_out(across, hops[k], sibling, across_send.at[k], 3 + k).start()
    gate_rows(chips - 1, 0)
    for block in (sibling, left + 1 - 2 * core, right + 1 - 2 * core):
        await_w_out(block, all_parts, 2)
    for k in range(2):
        await_w_out(across + 1 - 2 * core, hops[k], 3 + k)
    multiply(0, chips // 2)
    send_final(0, chips // 2)
    for bp in range(chips // 2, chips):
        multiply(bp, bp + 1)
        send_final(bp, bp + 1)

    places = [
        _dot(eye, _slot_onehot(row, nslot, part), ((1,), (1,))).astype(BF16) for part in range(2)
    ]
    at_owner = c == _owner(e, e, E, C)

    def await_final(k, carry):
        @pl.when(jnp.logical_not((k == e) & at_owner))
        def _():
            _drain(fin_dst.at[k], fin_recv.at[k])

        return carry

    lax.fori_loop(0, E, await_final, 0)
    for j in range(2):
        arrived = fin_dst[:, :, j * half_n : (j + 1) * half_n].reshape(nslot, half_n)
        for part in range(2):
            begin = part * half + j * half_n
            out[:, begin : begin + half_n] = _dot(places[part], arrived).astype(BF16)

    for h in range(2):
        _drain(stok.at[h, peers], tok_send.at[h])
        for k in range(3):
            _drain(rows.at[h, 0], row_send.at[h, k])
            _drain(rows.at[h, 0], fwd_send.at[h, k])
        _drain(rows.at[h, 0], hop_send.at[h])
    _drain(wstep_all.at[pl.ds(0, C - 1)], step_send)
    _drain(sss.at[peers], ss_send)
    _drain(ss.at[pl.ds(0, C - 1)], pos_send)
    for chip in range(chips):
        _drain(sback.at[chip, peers], back_send.at[chip])
    for bp in range(chips):
        _drain(gathered.at[bp, pl.ds(0, C - 1)], gated_send.at[bp])

    def left_final(k, carry):
        bp, q = k // (2 * group), lax.rem(k, 2 * group)

        @pl.when(jnp.logical_not((first_of(c) + q // 2 == e) & (2 * bp + lax.rem(q, 2) == c)))
        def _():
            _drain(fin_src.at[bp, q], fin_send.at[k])

        return carry

    lax.fori_loop(0, E, left_final, 0)
    for k, where in enumerate((first_part, first_part, last_part, last_part, all_parts) + hops + (all_parts,) * 2 + (next_part,) * 2):
        _drain(w_out.at[0, where], wout_send.at[k])
    for k in range(2):
        _drain(w_out.at[0, hops[k]], across_send.at[k])


def per_device(
    tokens,
    route,
    w_inner,
    w_state,
    w_step,
    step_bias,
    decay_log,
    skip_gain,
    conv_weight,
    conv_bias,
    w_out,
):
    T, width = tokens.shape[1:]
    E, C = lax.axis_size("expert"), lax.axis_size("context")
    chips = C // 2
    chans = w_inner.shape[3]
    wide = w_state.shape[2] + C * 16
    vmem = pl.BlockSpec(memory_space=pltpu.VMEM)
    hbm = pl.BlockSpec(memory_space=pl.ANY)
    dma = pltpu.SemaphoreType.DMA
    flat = pltpu.VMEM((chips, E, 16, chans), BF16)
    mixed = pl.pallas_call(
        functools.partial(layer_kernel, E, C),
        out_shape=jax.ShapeDtypeStruct((T, width), BF16),
        in_specs=[vmem, hbm, hbm, hbm, vmem, vmem, vmem, vmem, vmem, vmem, hbm],
        out_specs=vmem,
        scratch_shapes=[
            pltpu.VMEM((T, width), BF16),
            pltpu.VMEM(w_state.shape[1:], BF16),
            pltpu.VMEM((C, T), jnp.int32),
            pltpu.VMEM((2, width // 4, 2, chans), BF16),
            pltpu.VMEM((2, width, chans), BF16),
            pltpu.VMEM((C, chans, width), BF16),
            pltpu.VMEM((2, E, 16, width // 4), BF16),
            pltpu.VMEM((2, E, 16, width // 4), BF16),
            pltpu.VMEM((2, C, E * 8, width // 2), BF16),
            flat,
            flat,
            flat,
            flat,
            flat,
            pltpu.VMEM((C, 16, width), BF16),
            pltpu.VMEM((E, 16, wide // 2), BF16),
            pltpu.VMEM((E, 16, wide // 2), BF16),
            pltpu.VMEM((C, T, wide), BF16),
            pltpu.VMEM((chips, C, E // C, 16, chans), BF16),
            pltpu.VMEM((chips, 2 * (E // C), 16, width // 2), BF16),
            pltpu.VMEM((E, 16, width // 2), BF16),
            pltpu.VMEM((HEAD_DIM, chans), F32),
            pltpu.VMEM((8, chans), F32),
            pltpu.VMEM((2, T, chans), BF16),
            dma((2,)),
            dma((2,)),
            dma,
            dma((2,)),
            dma((2,)),
            dma,
            dma,
            dma((2, 3)),
            dma((2, C)),
            dma((2, 3)),
            dma((2,)),
            dma,
            dma,
            dma,
            dma,
            dma((chips,)),
            dma((chips,)),
            dma((11,)),
            dma((6, C)),
            dma((2,)),
            dma((chips,)),
            dma((chips,)),
            dma((chips,)),
            dma((chips,)),
            dma((E,)),
            dma((E,)),
        ],
        compiler_params=pltpu.CompilerParams(
            collective_id=0, has_side_effects=True, vmem_limit_bytes=VMEM_LIMIT
        ),
        name="layer",
    )(
        route[0, :, 0].reshape(C, T),
        tokens[0],
        w_inner[0],
        w_state[0],
        w_step[0].T,
        step_bias[None, :],
        decay_log[None, :],
        skip_gain[None, :],
        conv_weight,
        conv_bias[None, :],
        w_out[0],
    )
    return mixed[None]


def solution(mesh):
    in_specs = (
        P("expert", "context", None),
        P("expert", None, None),
        P("expert", None, None, "context"),
        P("expert", None, None),
        P("expert", None, "context"),
        P("context"),
        P("context"),
        P("context"),
        P(None, "context"),
        P("context"),
        P("expert", "context", None),
    )
    out_specs = P("expert", "context", None)
    return jax.shard_map(
        per_device, mesh=mesh, in_specs=in_specs, out_specs=out_specs, check_vma=False
    )
```
